256 devices in a mesh: ctx: 16 (over z, x_hi), tp: 4 (over y), dp: 4 (over x_lo, core).
Axes of the slice: x: 4 (x_hi: 2, x_lo: 2; x = x_hi * 2 + x_lo), y: 4, z: 8, core: 2. Of those that a mesh axis runs over, the one named last changes fastest.
Arguments:
- q_raw: bfloat16 [4, 4096, 4096], P('dp', 'ctx', 'tp'), may hold values from -6 to 6
- k_raw: bfloat16 [4, 4096, 4096], P('dp', 'ctx', 'tp'), may hold values from -6 to 6
- values: bfloat16 [4, 4096, 4096], P('dp', 'ctx', 'tp'), may hold values from -6 to 6
- d_out: bfloat16 [4, 4096, 4096], P('dp', 'ctx', 'tp'), may hold values from -6 to 6
- q_gain: float32 [32, 128], P('tp'), may hold values from 0.5 to 6
- k_gain: float32 [32, 128], P('tp'), may hold values from 0.5 to 6
- q_weight: bfloat16 [4096, 4096], P(None, 'tp'), may hold values from -0.09375 to 0.09375
- doc_lengths: int32 [4, 8], P('dp'), may hold values from 1 to 3840, as said below
Outputs:
- input_grad: bfloat16 [4, 4096, 4096], P('dp', 'ctx', 'tp')
- key_grad: bfloat16 [4, 4096, 4096], P('dp', 'ctx', 'tp')
- value_grad: bfloat16 [4, 4096, 4096], P('dp', 'ctx', 'tp')
- q_gain_grad: float32 [32, 128], P('tp')
- k_gain_grad: float32 [32, 128], P('tp')
The draws below stay inside these ranges and needn't reach their ends.
Inputs may be any that keep to these rules, and one draw needn't show every extreme that they name: `doc_lengths`: each sequence's lengths sum to 4096.
All inputs are finite; a program needn't handle non-finite values.
Results may differ from the reference program's by a relative error of at most 0.02.
The reference program's roundings to bfloat16 on the way count: a program that leaves them out, or rounds other values in their place, can miss the bound.
Values may be sent and summed in bfloat16 or wider, within the bound.
No kernel may reach another device: no remote copies, remote signals or barrier semaphores. Data moves between devices by JAX's collectives and lax.ppermute only.
A program may use at most 128 MiB of HBM per device.

```python
import jax
import jax.numpy as jnp
from jax import lax

D = 4096
HEADS = 32
HD = 128
TOK_DEV = 256
NDOCS = 8
SEQ = 4096
SEQS = 4
N_CTX = 16


def key_field(key):
    return jnp.clip(jax.random.normal(jax.random.fold_in(key, 17), (SEQS, SEQ, HEADS * HD), jnp.float32), -6.0, 6.0)


def draw_k_raw(key, part):
    base = key_field(key)
    return base.astype(jnp.bfloat16)


def draw_q_raw(key, part):
    base = key_field(key)
    key = jax.random.fold_in(key, 3)
    return jnp.clip(jax.random.normal(key, base.shape, jnp.float32), -6.0, 6.0).astype(jnp.bfloat16)


def draw_q_gain(key, part):
    key = jax.random.fold_in(key, 5)
    return jax.random.uniform(key, (HEADS, HD), jnp.float32, 0.5, 2.5)


def draw_k_gain(key, part):
    key = jax.random.fold_in(key, 7)
    return jax.random.uniform(key, (HEADS, HD), jnp.float32, 0.5, 2.5)


def split_total(key, total, pieces):
    order = jax.random.permutation(key, total - 1) + 1
    cuts = jnp.sort(order[:pieces - 1]).astype(jnp.int32)
    edges = jnp.concatenate([jnp.zeros((1,), jnp.int32), cuts, jnp.full((1,), total, jnp.int32)])
    return (edges[1:] - edges[:-1]).astype(jnp.int32)


def draw_doc_lengths(key, part):
    key = jax.random.fold_in(key, 11)
    margin = TOK_DEV // 2
    leading = (NDOCS - 1) // 2
    trailing = NDOCS - 1 - leading
    rows = []
    for member in range(SEQS):
        member_key = jax.random.fold_in(key, member)
        front = split_total(jax.random.fold_in(member_key, 1), margin, leading)
        back = split_total(jax.random.fold_in(member_key, 2), margin, trailing)
        middle = jnp.full((1,), SEQ - 2 * margin, jnp.int32)
        rows.append(jnp.concatenate([front, middle, back]))
    return jnp.stack(rows).astype(jnp.int32)


def shard_levels(stream_key, extent, cuts, least, high):
    def one(position, blocks):
        draws = jax.random.uniform(jax.random.fold_in(jax.random.fold_in(stream_key, 6), position), (blocks,), jnp.float32, least / len(cuts), high / len(cuts))
        return jnp.repeat(jnp.exp(draws), extent[position] // blocks).reshape((-1,) + (1,) * (len(extent) - position - 1))

    level = one(*cuts[0])
    for cut in cuts[1:]:
        level = level * one(*cut)
    return level


def noise(stream_key, shape, spread, most, cuts=(), held_as=jnp.bfloat16):
    level = shard_levels(stream_key, shape, cuts, -0.22, 0.18) if cuts else 1.0
    result = jax.random.normal(stream_key, shape, jnp.float32) * spread * level
    return jnp.minimum(jnp.maximum(result, -most), most).astype(held_as)


def setup_inputs(seed: int = 0) -> dict:
    key_list = jax.random.split(jax.random.key(seed), 9)
    q_raw = draw_q_raw(jax.random.fold_in(key_list[8], 71), 0)
    k_raw = draw_k_raw(jax.random.fold_in(key_list[8], 71), 0)
    values = noise(key_list[2], (SEQS, SEQ, HEADS * HD), 1.0, 6.0, ((0, 4), (1, 16), (2, 4)))
    d_out = noise(key_list[3], (SEQS, SEQ, HEADS * HD), 1.0, 6.0, ((0, 4), (1, 16), (2, 4)))
    q_gain = draw_q_gain(jax.random.fold_in(key_list[8], 71), 0)
    k_gain = draw_k_gain(jax.random.fold_in(key_list[8], 71), 0)
    q_weight = noise(key_list[6], (D, HEADS * HD), D ** -0.5, 0.09375, ((1, 4),))
    doc_lengths = draw_doc_lengths(jax.random.fold_in(key_list[8], 71), 0)
    return dict(q_raw=q_raw, k_raw=k_raw, values=values, d_out=d_out, q_gain=q_gain, k_gain=k_gain, q_weight=q_weight, doc_lengths=doc_lengths)


NORM_EPSILON = 1e-05
MASKED_SCORE = -1e+30

def norm_forward(raw_rows, gain):
    row_count = raw_rows.shape[0]
    head_count, head_width = gain.shape
    widened = raw_rows.astype(jnp.float32).reshape(row_count, head_count, head_width)
    centered = widened - lax.optimization_barrier(jnp.mean(widened, axis=2, keepdims=True))
    inverse = lax.rsqrt(lax.optimization_barrier(jnp.mean(centered * centered, axis=2, keepdims=True)) + NORM_EPSILON)
    unit_rows = centered * inverse
    scaled = (unit_rows * gain[None]).astype(jnp.bfloat16)
    return (unit_rows, inverse, scaled.reshape(row_count, head_count * head_width))

def norm_backward(grad_norm, unit_rows, inverse, gain):
    scaled = grad_norm * gain[None]
    mean_grad = lax.optimization_barrier(jnp.mean(scaled, axis=2, keepdims=True))
    mean_cross = lax.optimization_barrier(jnp.mean(scaled * unit_rows, axis=2, keepdims=True))
    raw_grad = (scaled - mean_grad - unit_rows * mean_cross) * inverse
    return (raw_grad, lax.optimization_barrier(jnp.sum(grad_norm * unit_rows, axis=0)))

def doc_index(positions, starts):
    return lax.optimization_barrier(jnp.sum((positions[:, None] >= starts[None, :]).astype(jnp.int32), axis=1)) - 1

def shard_sum(pieces):
    rounded = lax.optimization_barrier(pieces.astype(jnp.bfloat16))
    return lax.optimization_barrier(jnp.sum(rounded.astype(jnp.float32), axis=0))

def reference(q_raw, k_raw, values, d_out, q_gain, k_gain, q_weight, doc_lengths):
    factor = HD ** (-0.5)
    positions = jnp.arange(SEQ, dtype=jnp.int32)
    inputs_out = []
    keys_out = []
    values_out = []
    q_gain_grad = jnp.zeros((HEADS, HD), jnp.float32)
    k_gain_grad = jnp.zeros((HEADS, HD), jnp.float32)
    for member in range(SEQS):
        lengths = doc_lengths[member].astype(jnp.int32)
        starts = (jnp.cumsum(lengths) - lengths).astype(jnp.int32)
        docs = doc_index(positions, starts)
        pair_mask = (docs[:, None] == docs[None, :]) & (positions[None, :] <= positions[:, None])
        q_unit, q_inverse, q_norm = norm_forward(q_raw[member], q_gain)
        k_unit, k_inverse, k_norm = norm_forward(k_raw[member], k_gain)

        def per_head(operands):
            query_head, key_head, value_head, grad_head = operands
            scores = jnp.dot(query_head, key_head.T, preferred_element_type=jnp.float32) * factor
            scores = jnp.where(pair_mask, scores, MASKED_SCORE)
            row_peak = lax.optimization_barrier(jnp.max(scores, axis=1))
            shifted = jnp.where(pair_mask, jnp.exp(scores - row_peak[:, None]), 0.0)
            row_total = lax.optimization_barrier(jnp.sum(shifted, axis=1))
            dot_terms = jnp.dot(grad_head, value_head.T, preferred_element_type=jnp.float32)
            log_total = row_peak + jnp.log(row_total)
            row_delta = lax.optimization_barrier(jnp.sum(shifted * dot_terms, axis=1)) / row_total
            chances = jnp.where(pair_mask, jnp.exp(scores - log_total[:, None]), 0.0)
            score_grad = (chances * (dot_terms - row_delta[:, None]) * factor).astype(jnp.bfloat16)
            chance_rounded = chances.astype(jnp.bfloat16)
            by_query = score_grad.astype(jnp.float32).reshape(N_CTX, TOK_DEV, SEQ)
            value_part = shard_sum(jnp.einsum('cqk,cqd->ckd', chance_rounded.astype(jnp.float32).reshape(N_CTX, TOK_DEV, SEQ), grad_head.astype(jnp.float32).reshape(N_CTX, TOK_DEV, HD)))
            key_part = shard_sum(jnp.einsum('cqk,cqd->ckd', by_query, query_head.astype(jnp.float32).reshape(N_CTX, TOK_DEV, HD)))
            query_part = shard_sum(jnp.einsum('qck,ckd->cqd', score_grad.astype(jnp.float32).reshape(SEQ, N_CTX, TOK_DEV), key_head.astype(jnp.float32).reshape(N_CTX, TOK_DEV, HD)))
            return (query_part, key_part, value_part)

        def heads_first(rows):
            return rows.reshape(SEQ, HEADS, HD).transpose(1, 0, 2)
        query_grads, key_grads, value_sums = lax.map(per_head, (heads_first(q_norm), heads_first(k_norm), heads_first(values[member]), heads_first(d_out[member])))
        query_norm_grad = query_grads.transpose(1, 0, 2)
        key_norm_grad = key_grads.transpose(1, 0, 2)
        q_raw_grad, q_gain_part = norm_backward(query_norm_grad, q_unit, q_inverse, q_gain)
        k_raw_grad, k_gain_part = norm_backward(key_norm_grad, k_unit, k_inverse, k_gain)
        q_gain_grad = q_gain_grad + q_gain_part
        k_gain_grad = k_gain_grad + k_gain_part
        q_rows = q_raw_grad.reshape(SEQ, HEADS * HD).astype(jnp.bfloat16)
        inputs_out.append(jnp.dot(q_rows, q_weight.T, preferred_element_type=jnp.float32).astype(jnp.bfloat16))
        keys_out.append(k_raw_grad.reshape(SEQ, HEADS * HD).astype(jnp.bfloat16))
        values_out.append(value_sums.transpose(1, 0, 2).reshape(SEQ, HEADS * HD).astype(jnp.bfloat16))
    return (jnp.stack(inputs_out), jnp.stack(keys_out), jnp.stack(values_out), q_gain_grad, k_gain_grad)
```

```python
import functools

import jax
import jax.numpy as jnp
from jax import lax
from jax.experimental import pallas as pl
from jax.experimental.pallas import tpu as pltpu
from jax.sharding import PartitionSpec as P

NORM_EPSILON = 1e-05
MASKED_SCORE = -1e30
HEADS_LOCAL = 8
HD = 128
ROWS = 256
LANES = 256
CHUNKS = 2
FACTOR = HD ** (-0.5)
EXP2_FACTOR = FACTOR * 1.4426950408889634
VMEM_LIMIT = 40 * 1024 * 1024

Z_GROUPS = [[2 * z + half for z in range(8)] for half in range(2)]
HALF_SWAP = [(index, index ^ 1) for index in range(16)]


def nt_dot(a, b):
    return lax.dot_general(a, b, (((1,), (1,)), ((), ())), preferred_element_type=jnp.float32)


def nn_dot(a, b):
    return lax.dot_general(a, b, (((1,), (0,)), ((), ())), preferred_element_type=jnp.float32)


def unit_norm(raw):
    widened = raw.astype(jnp.float32)
    centered = widened - jnp.mean(widened, axis=1, keepdims=True)
    inverse = lax.rsqrt(jnp.mean(centered * centered, axis=1, keepdims=True) + NORM_EPSILON)
    return centered * inverse, inverse


def unit_norm_backward(grad_norm, unit_rows, inverse, gain):
    scaled = grad_norm * gain
    mean_grad = jnp.mean(scaled, axis=1, keepdims=True)
    mean_cross = jnp.mean(scaled * unit_rows, axis=1, keepdims=True)
    return (scaled - mean_grad - unit_rows * mean_cross) * inverse


def key_prep_kernel(raw_ref, gain_ref, norm_ref, norm_t_ref):
    unit_rows, _ = unit_norm(raw_ref[0])
    scaled = unit_rows * gain_ref[...]
    norm_ref[0] = scaled.astype(jnp.bfloat16)
    norm_t_ref[0] = scaled.T.astype(jnp.bfloat16)


def key_prep(raw, gain):
    count = raw.shape[0]
    return pl.pallas_call(
        key_prep_kernel,
        grid=(count,),
        in_specs=[
            pl.BlockSpec((1, ROWS, HD), lambda i: (i, 0, 0)),
            pl.BlockSpec((1, HD), lambda i: (0, 0)),
        ],
        out_specs=[
            pl.BlockSpec((1, ROWS, HD), lambda i: (i, 0, 0)),
            pl.BlockSpec((1, HD, ROWS), lambda i: (i, 0, 0)),
        ],
        out_shape=[
            jax.ShapeDtypeStruct((count, ROWS, HD), jnp.bfloat16),
            jax.ShapeDtypeStruct((count, HD, ROWS), jnp.bfloat16),
        ],
        cost_estimate=pl.CostEstimate(flops=0, bytes_accessed=3 * 2**19, transcendentals=0),
        name="key_prep",
    )(raw, gain)


def fold(tile):
    return tile.reshape(tile.shape[0] // 8, 8, tile.shape[1])


def attention_kernel(
    has_prior,
    bounds_ref,
    half_ref,
    pos_ref,
    low_ref,
    query_ref,
    grad_ref,
    norm_own,
    norm_other,
    norm_t_own,
    norm_t_other,
    value_own,
    value_other,
    gain_ref,
    *rest,
):
    if has_prior:
        prior, rest = rest[:4], rest[4:]
    dq_ref, gain_grad_ref, dk_own, dk_other, dv_own, dv_other, score_ref, dot_ref, dqt_ref = rest
    blocks = query_ref.shape[0] // LANES
    half = half_ref[0]
    if has_prior:
        for target, source in zip((dk_own, dk_other, dv_own, dv_other), prior):
            target[...] = source[...]
    else:
        for target in (dk_own, dk_other, dv_own, dv_other):
            target[...] = jnp.zeros_like(target)
    gain_grad_ref[...] = jnp.zeros_like(gain_grad_ref)
    sides = (
        (norm_own, norm_t_own, value_own, dk_own, dv_own),
        (norm_other, norm_t_other, value_other, dk_other, dv_other),
    )

    def block_body(block, carry):
        rows = pl.ds(pl.multiple_of(block * LANES, LANES), LANES)
        unit_rows, inverse = unit_norm(query_ref[rows, :])
        query = (unit_rows * gain_ref[...]).astype(jnp.bfloat16)
        grad = grad_ref[rows, :]
        pos = pos_ref[pl.ds(block, 1), :]
        low = low_ref[pl.ds(block, 1), :]
        first, inner, diagonal, last = (bounds_ref[block, i] for i in range(4))

        def scores_body(masked, tile, peak):
            for side, (norm, _, value, _, _) in enumerate(sides):
                scores = nt_dot(norm[tile], query)
                if masked:
                    which = half if side == 0 else 1 - half
                    key_pos = (2 * tile + which) * ROWS + lax.broadcasted_iota(
                        jnp.int32, (ROWS, LANES), 0
                    )
                    scores = jnp.where(
                        (key_pos >= low) & (key_pos <= pos), scores, MASKED_SCORE
                    )
                score_ref[2 * tile + side] = scores
                peak = jnp.maximum(peak, jnp.max(fold(scores), axis=0))
                dot_ref[2 * tile + side] = nt_dot(value[tile], grad)
            return peak

        peak = jnp.full((8, LANES), MASKED_SCORE, jnp.float32)
        peak = lax.fori_loop(first, inner, functools.partial(scores_body, True), peak)
        peak = lax.fori_loop(inner, diagonal, functools.partial(scores_body, False), peak)
        peak = lax.fori_loop(diagonal, last, functools.partial(scores_body, True), peak)
        peak = jnp.max(peak, axis=0, keepdims=True) * EXP2_FACTOR

        def exp_body(tile, sums):
            total, weighted = sums
            for side in range(2):
                shifted = jnp.exp2(score_ref[2 * tile + side] * EXP2_FACTOR - peak)
                score_ref[2 * tile + side] = shifted
                total = total + jnp.sum(fold(shifted), axis=0)
                weighted = weighted + jnp.sum(fold(shifted * dot_ref[2 * tile + side]), axis=0)
            return total, weighted

        empty = jnp.zeros((8, LANES), jnp.float32)
        total, weighted = lax.fori_loop(first, last, exp_body, (empty, empty))
        share = 1.0 / jnp.sum(total, axis=0, keepdims=True)
        delta = jnp.sum(weighted, axis=0, keepdims=True) * share
        dqt_ref[...] = jnp.zeros_like(dqt_ref)

        def grads_body(tile, carry):
            for side, (_, norm_t, _, dk, dv) in enumerate(sides):
                chance = score_ref[2 * tile + side] * share
                score_grad = (chance * (dot_ref[2 * tile + side] - delta)).astype(jnp.bfloat16)
                dv[tile] += nn_dot(chance.astype(jnp.bfloat16), grad)
                dk[tile] += nn_dot(score_grad, query)
                dqt_ref[...] += nn_dot(norm_t[tile], score_grad)
            return carry

        lax.fori_loop(first, last, grads_body, 0)
        query_grad = dqt_ref[...].T * FACTOR
        dq_ref[rows, :] = unit_norm_backward(
            query_grad, unit_rows, inverse, gain_ref[...]
        ).astype(jnp.bfloat16)
        gain_grad_ref[...] += jnp.sum(query_grad * unit_rows, axis=0, keepdims=True)
        return carry

    lax.fori_loop(0, blocks, block_body, 0)


def attention(bounds, half, pos, low, query, grad, keys, values, gain, prior):
    rows = query.shape[0]
    tiles = keys[0][0].shape[0]
    smem = pl.BlockSpec(memory_space=pltpu.SMEM)
    vmem = pl.BlockSpec(memory_space=pltpu.VMEM)
    wide = jax.ShapeDtypeStruct((tiles, ROWS, HD), jnp.float32)
    operands = [
        bounds, half, pos, low, query, grad,
        keys[0][0], keys[1][0], keys[0][1], keys[1][1], values[0], values[1], gain,
    ]
    if prior is not None:
        operands += list(prior)
    flops = 5 * 2 * rows * tiles * ROWS * HD
    return pl.pallas_call(
        functools.partial(attention_kernel, prior is not None),
        in_specs=[smem, smem] + [vmem] * (len(operands) - 2),
        out_specs=[vmem] * 6,
        out_shape=[
            jax.ShapeDtypeStruct((rows, HD), jnp.bfloat16),
            jax.ShapeDtypeStruct((1, HD), jnp.float32),
            wide, wide, wide, wide,
        ],
        scratch_shapes=[
            pltpu.VMEM((2 * tiles, ROWS, LANES), jnp.float32),
            pltpu.VMEM((2 * tiles, ROWS, LANES), jnp.float32),
            pltpu.VMEM((HD, LANES), jnp.float32),
        ],
        compiler_params=pltpu.CompilerParams(vmem_limit_bytes=VMEM_LIMIT),
        cost_estimate=pl.CostEstimate(
            flops=2 * flops, bytes_accessed=2**24, transcendentals=rows * tiles * ROWS
        ),
        name="attention",
    )(*operands)


def key_finish_kernel(own_ref, other_ref, raw_ref, gain_ref, out_ref, gain_grad_ref):
    @pl.when(pl.program_id(0) == 0)
    def _():
        gain_grad_ref[...] = jnp.zeros_like(gain_grad_ref)

    grad_norm = (own_ref[0] + other_ref[0].astype(jnp.float32)) * FACTOR
    unit_rows, inverse = unit_norm(raw_ref[0])
    out_ref[0] = unit_norm_backward(grad_norm, unit_rows, inverse, gain_ref[...]).astype(
        jnp.bfloat16
    )
    gain_grad_ref[...] += jnp.sum(grad_norm * unit_rows, axis=0, keepdims=True)


def key_finish(own, other, raw, gain):
    count = raw.shape[0]
    block = pl.BlockSpec((1, ROWS, HD), lambda i: (i, 0, 0))
    row = pl.BlockSpec((1, HD), lambda i: (0, 0))
    return pl.pallas_call(
        key_finish_kernel,
        grid=(count,),
        in_specs=[block, block, block, row],
        out_specs=[block, row],
        out_shape=[
            jax.ShapeDtypeStruct((count, ROWS, HD), jnp.bfloat16),
            jax.ShapeDtypeStruct((1, HD), jnp.float32),
        ],
        cost_estimate=pl.CostEstimate(flops=0, bytes_accessed=5 * 2**19, transcendentals=0),
        name="key_finish",
    )(own, other, raw, gain)


def project_kernel(rows_ref, weight_ref, out_ref, joined_ref):
    @pl.when(pl.program_id(0) == 0)
    def _():
        for head in range(rows_ref.shape[0]):
            joined_ref[:, head * HD : (head + 1) * HD] = rows_ref[head]

    out_ref[0] = nt_dot(joined_ref[...], weight_ref[...]).astype(jnp.bfloat16)


def project(rows, weight, parts):
    heads, count, _ = rows.shape
    model, inner = weight.shape
    width = model // parts
    block = 512
    per_part = width // block
    return pl.pallas_call(
        project_kernel,
        grid=(model // block,),
        in_specs=[
            pl.BlockSpec((heads, count, HD), lambda i: (0, 0, 0)),
            pl.BlockSpec((block, inner), lambda i: (i, 0)),
        ],
        out_specs=pl.BlockSpec((1, count, block), lambda i: (i // per_part, 0, i % per_part)),
        out_shape=jax.ShapeDtypeStruct((parts, count, width), jnp.bfloat16),
        scratch_shapes=[pltpu.VMEM((count, inner), jnp.bfloat16)],
        cost_estimate=pl.CostEstimate(
            flops=2 * count * model * inner, bytes_accessed=2 * model * inner, transcendentals=0
        ),
        name="project",
    )(rows, weight)


def along_z(pieces):
    return lax.all_to_all(pieces, "ctx", 0, 0, axis_index_groups=Z_GROUPS)


def swap_half(piece):
    return lax.ppermute(piece, "ctx", HALF_SWAP)


def by_head(rows):
    return rows.reshape(rows.shape[0], HEADS_LOCAL, HD).transpose(1, 0, 2)


def by_row(pieces):
    return pieces.transpose(1, 0, 2).reshape(pieces.shape[1], HEADS_LOCAL * HD)


def reduce_tp(parts):
    count = parts.shape[0]
    me = lax.axis_index("tp")

    def part(step):
        return lax.dynamic_index_in_dim(parts, lax.rem(me + step, count), 0, False)

    total = part(0).astype(jnp.float32)
    for step in range(1, count):
        moved = lax.ppermute(part(step), "tp", [(i, (i + step) % count) for i in range(count)])
        total = total + moved.astype(jnp.float32)
    return total.astype(jnp.bfloat16)


def spread_gains(gains, z):
    mine = jnp.arange(HEADS_LOCAL, dtype=jnp.int32)[:, None, None] == z
    total = jnp.where(mine, gains[None], 0.0)
    for distance in (1, 2):
        total = total + lax.ppermute(total, "dp", [(i, i ^ distance) for i in range(4)])
    for distance in (1, 2, 4, 8):
        total = total + lax.ppermute(total, "ctx", [(i, i ^ distance) for i in range(16)])
    return total


def local(q_raw, k_raw, values, d_out, q_gain, k_gain, q_weight, doc_lengths):
    ctx = lax.axis_index("ctx")
    z = ctx // 2
    half = lax.rem(ctx, 2)
    lengths = doc_lengths[0]
    starts = jnp.cumsum(lengths) - lengths
    q_gain_row = lax.dynamic_slice_in_dim(q_gain, z, 1, 0)
    k_gain_row = lax.dynamic_slice_in_dim(k_gain, z, 1, 0)

    key_own = along_z(by_head(k_raw[0]))
    value_own = along_z(by_head(values[0]))
    key_other = swap_half(key_own)
    value_other = swap_half(value_own)
    keys = (key_prep(key_own, k_gain_row), key_prep(key_other, k_gain_row))

    count = ROWS // CHUNKS
    prior = None
    query_gain_sum = jnp.zeros((1, HD), jnp.float32)
    input_parts = []
    for chunk in range(CHUNKS):
        rows = slice(chunk * count, (chunk + 1) * count)
        sent = jnp.stack([by_head(q_raw[0, rows]), by_head(d_out[0, rows])], axis=1)
        moved = along_z(sent)
        query = moved[:, 0].reshape(8 * count, HD)
        grad = moved[:, 1].reshape(8 * count, HD)
        pos = (
            (2 * jnp.arange(8, dtype=jnp.int32) + half)[:, None] * ROWS
            + chunk * count
            + jnp.arange(count, dtype=jnp.int32)[None, :]
        ).reshape(8 * count // LANES, LANES)
        low = jnp.max(
            jnp.where(starts[None, None, :] <= pos[:, :, None], starts[None, None, :], 0), axis=2
        )
        first = low[:, 0] // (2 * ROWS)
        last = pos[:, -1] // (2 * ROWS) + 1
        inner = jnp.clip((low[:, -1] + 2 * ROWS - 1) // (2 * ROWS), first, last)
        diagonal = jnp.clip(pos[:, 0] // (2 * ROWS), inner, last)
        bounds = jnp.stack([first, inner, diagonal, last], axis=1).astype(jnp.int32)
        dq, gain_part, *prior = attention(
            bounds,
            half.reshape(1),
            pos,
            low,
            query,
            grad,
            keys,
            (value_own, value_other),
            q_gain_row,
            prior,
        )
        query_gain_sum = query_gain_sum + gain_part
        returned = along_z(dq.reshape(8, count, HD))
        input_parts.append(reduce_tp(project(returned, q_weight, 4)))
    dk_own, dk_other, dv_own, dv_other = prior

    dv_moved = swap_half(dv_other.astype(jnp.bfloat16))
    dk_moved = swap_half(dk_other.astype(jnp.bfloat16))
    value_sum = (dv_own + dv_moved.astype(jnp.float32)).astype(jnp.bfloat16)
    value_grad = by_row(along_z(value_sum))
    dk_raw, key_gain_sum = key_finish(dk_own, dk_moved, key_own, k_gain_row)
    key_grad = by_row(along_z(dk_raw))
    gains = spread_gains(jnp.concatenate([query_gain_sum, key_gain_sum], axis=0), z)
    input_grad = jnp.concatenate(input_parts, axis=0)
    return (input_grad[None], key_grad[None], value_grad[None], gains[:, 0], gains[:, 1])


def solution(mesh):
    return jax.shard_map(
        local,
        mesh=mesh,
        in_specs=(
            P("dp", "ctx", "tp"),
            P("dp", "ctx", "tp"),
            P("dp", "ctx", "tp"),
            P("dp", "ctx", "tp"),
            P("tp", None),
            P("tp", None),
            P(None, "tp"),
            P("dp", None),
        ),
        out_specs=(
            P("dp", "ctx", "tp"),
            P("dp", "ctx", "tp"),
            P("dp", "ctx", "tp"),
            P("tp", None),
            P("tp", None),
        ),
        check_vma=False,
    )
```

```python
import functools

import jax
import jax.numpy as jnp
from jax import lax
from jax.experimental import pallas as pl
from jax.experimental.pallas import tpu as pltpu
from jax.sharding import PartitionSpec as P

NORM_EPSILON = 1e-05
MASKED_SCORE = -1e30
HEADS_LOCAL = 8
HD = 128
ROWS = 256
LANES = 256
PAIRS = 2
FACTOR = HD ** (-0.5)
EXP2_FACTOR = FACTOR * 1.4426950408889634
VMEM_LIMIT = 60 * 1024 * 1024

DEPTH = 8
Z_GROUPS = [[2 * z + half for z in range(8)] for half in range(2)]
HALF_SWAP = [(index, index ^ 1) for index in range(16)]


def nt_dot(a, b):
    return lax.dot_general(a, b, (((1,), (1,)), ((), ())), preferred_element_type=jnp.float32)


def nn_dot(a, b):
    return lax.dot_general(a, b, (((1,), (0,)), ((), ())), preferred_element_type=jnp.float32)


def unit_norm(raw):
    widened = raw.astype(jnp.float32)
    centered = widened - jnp.mean(widened, axis=1, keepdims=True)
    inverse = lax.rsqrt(jnp.mean(centered * centered, axis=1, keepdims=True) + NORM_EPSILON)
    return centered * inverse, inverse


def unit_norm_backward(grad_norm, unit_rows, inverse, gain):
    scaled = grad_norm * gain
    mean_grad = jnp.mean(scaled, axis=1, keepdims=True)
    mean_cross = jnp.mean(scaled * unit_rows, axis=1, keepdims=True)
    return (scaled - mean_grad - unit_rows * mean_cross) * inverse


VMEM_SPEC = pl.BlockSpec(memory_space=pltpu.VMEM)
SMEM_SPEC = pl.BlockSpec(memory_space=pltpu.SMEM)
ANY_SPEC = pl.BlockSpec(memory_space=pltpu.HBM)


def pack_kernel(first_ref, second_ref, out_ref, held_ref, in_sem, out_sem):
    def inward(head, which):
        return pltpu.make_async_copy(
            (first_ref, second_ref)[which].at[:, head * HD : (head + 1) * HD],
            held_ref.at[head, which],
            in_sem.at[head, which],
        )

    def outward(head):
        return pltpu.make_async_copy(held_ref.at[head], out_ref.at[head], out_sem.at[head])

    for head in range(HEADS_LOCAL):
        for which in range(2):
            inward(head, which).start()
    for head in range(HEADS_LOCAL):
        for which in range(2):
            inward(head, which).wait()
        outward(head).start()
    for head in range(HEADS_LOCAL):
        outward(head).wait()


def pack(first, second):
    shape = (HEADS_LOCAL, 2, ROWS, HD)
    return pl.pallas_call(
        pack_kernel,
        in_specs=[ANY_SPEC, ANY_SPEC],
        out_specs=ANY_SPEC,
        out_shape=jax.ShapeDtypeStruct(shape, jnp.bfloat16),
        scratch_shapes=[
            pltpu.VMEM(shape, jnp.bfloat16),
            pltpu.SemaphoreType.DMA((HEADS_LOCAL, 2)),
            pltpu.SemaphoreType.DMA((HEADS_LOCAL,)),
        ],
        cost_estimate=pl.CostEstimate(flops=0, bytes_accessed=2**22, transcendentals=0),
        name="pack",
    )(first, second)


def unpack_kernel(pieces_ref, *refs):
    outs, (held_ref, in_sem, out_sem) = refs[:2], refs[2:]

    def inward(head):
        return pltpu.make_async_copy(pieces_ref.at[head], held_ref.at[head], in_sem.at[head])

    def outward(head, which):
        return pltpu.make_async_copy(
            held_ref.at[head, which * ROWS : (which + 1) * ROWS],
            outs[which].at[:, head * HD : (head + 1) * HD],
            out_sem.at[head, which],
        )

    for head in range(HEADS_LOCAL):
        inward(head).start()
    for head in range(HEADS_LOCAL):
        inward(head).wait()
        for which in range(2):
            outward(head, which).start()
    for head in range(HEADS_LOCAL):
        for which in range(2):
            outward(head, which).wait()


def unpack(pieces):
    rows = jax.ShapeDtypeStruct((ROWS, HEADS_LOCAL * HD), jnp.bfloat16)
    return pl.pallas_call(
        unpack_kernel,
        in_specs=[ANY_SPEC],
        out_specs=[ANY_SPEC, ANY_SPEC],
        out_shape=[rows, rows],
        scratch_shapes=[
            pltpu.VMEM(pieces.shape, jnp.bfloat16),
            pltpu.SemaphoreType.DMA((HEADS_LOCAL,)),
            pltpu.SemaphoreType.DMA((HEADS_LOCAL, 2)),
        ],
        cost_estimate=pl.CostEstimate(flops=0, bytes_accessed=2**22, transcendentals=0),
        name="unpack",
    )(pieces)


def whole(*shape):
    return pl.BlockSpec(shape, lambda i: (0,) * len(shape))


def key_prep_kernel(gain_ref, raw_ref, norm_ref, turned_ref, held_raw, held_norm, held_turned, in_sem, out_sem):
    inward = [
        pltpu.make_async_copy(raw_ref.at[tile, 0], held_raw.at[tile], in_sem.at[tile])
        for tile in range(DEPTH)
    ]
    outward = [
        pltpu.make_async_copy(held_norm, norm_ref, out_sem.at[0]),
        pltpu.make_async_copy(held_turned, turned_ref, out_sem.at[1]),
    ]
    for copy in inward:
        copy.start()
    for tile in range(DEPTH):
        inward[tile].wait()
        unit_rows, _ = unit_norm(held_raw[tile])
        scaled = unit_rows * gain_ref[...]
        held_norm[tile] = scaled.astype(jnp.bfloat16)
        held_turned[tile] = scaled.T.astype(jnp.bfloat16)
    for copy in outward:
        copy.start()
    for copy in outward:
        copy.wait()


def key_prep(gain, keys_values):
    shapes = [(DEPTH, ROWS, HD), (DEPTH, HD, ROWS)]
    return pl.pallas_call(
        key_prep_kernel,
        in_specs=[VMEM_SPEC, ANY_SPEC],
        out_specs=[ANY_SPEC] * 2,
        out_shape=[jax.ShapeDtypeStruct(shape, jnp.bfloat16) for shape in shapes],
        scratch_shapes=[
            pltpu.VMEM(shapes[0], jnp.bfloat16),
            pltpu.VMEM(shapes[0], jnp.bfloat16),
            pltpu.VMEM(shapes[1], jnp.bfloat16),
            pltpu.SemaphoreType.DMA((DEPTH,)),
            pltpu.SemaphoreType.DMA((2,)),
        ],
        cost_estimate=pl.CostEstimate(flops=0, bytes_accessed=2**22, transcendentals=0),
        name="key_prep",
    )(gain, keys_values)


def fold(tile):
    return tile.reshape(tile.shape[0] // 8, 8, tile.shape[1])


def attention_kernel(bounds_ref, half_ref, pos_ref, low_ref, gain_ref, *refs):
    queries_grads_ref, refs = refs[0], refs[1:]
    norms, turned, raws = refs[0:2], refs[2:4], refs[4:6]
    refs = refs[6:]
    dq_ref, gain_grad_ref, own_ref, other_ref = refs[:4]
    (
        chance_ref,
        dot_ref,
        peak_ref,
        dk_ref,
        dv_ref,
        dqt_ref,
        held_norm,
        held_turned,
        held_value,
        held_query,
        held_dq,
        cast_ref,
        in_sem,
        out_sem,
    ) = refs[4:]
    half = half_ref[0]
    moves = [(queries_grads_ref, held_query)]
    for side in range(2):
        moves.append((norms[side], held_norm.at[side]))
        moves.append((turned[side], held_turned.at[side]))
        moves.append((raws[side].at[:, 1], held_value.at[side]))
    loads = [
        pltpu.make_async_copy(source, target, in_sem.at[index])
        for index, (source, target) in enumerate(moves)
    ]
    for copy in loads:
        copy.start()
    dk_ref[...] = jnp.zeros_like(dk_ref)
    dv_ref[...] = jnp.zeros_like(dv_ref)
    gain_grad_ref[...] = jnp.zeros_like(gain_grad_ref)
    for copy in loads:
        copy.wait()

    def block_body(block, carry):
        unit_rows, inverse = unit_norm(held_query[block, 0])
        query = (unit_rows * gain_ref[...]).astype(jnp.bfloat16)
        grad = held_query[block, 1]
        pos = pos_ref[pl.ds(block, 1), :]
        low = low_ref[pl.ds(block, 1), :]
        first, inner, diagonal, last = (bounds_ref[block, i] for i in range(4))

        def scores_body(masked, step, sums):
            best, total, weighted = sums
            parts = []
            peak = jnp.full((8, LANES), MASKED_SCORE, jnp.float32)
            for pair in range(PAIRS):
                tile = step * PAIRS + pair
                for side in range(2):
                    scores = nt_dot(held_norm[side, tile], query)
                    mask = None
                    if masked:
                        which = half if side == 0 else 1 - half
                        key_pos = (2 * tile + which) * ROWS + lax.broadcasted_iota(
                            jnp.int32, (ROWS, LANES), 0
                        )
                        mask = (key_pos >= low) & (key_pos <= pos)
                        scores = jnp.where(mask, scores, MASKED_SCORE)
                    parts.append((tile, side, scores, mask))
                    peak = jnp.maximum(peak, jnp.max(fold(scores), axis=0))
            new_best = jnp.maximum(best, jnp.max(peak, axis=0, keepdims=True) * EXP2_FACTOR)
            scale = jnp.exp2(best - new_best)
            total, weighted = total * scale, weighted * scale
            for tile, side, scores, mask in parts:
                shifted = jnp.exp2(scores * EXP2_FACTOR - new_best)
                if masked:
                    shifted = jnp.where(mask, shifted, 0.0)
                dots = nt_dot(held_value[side, tile], grad)
                chance_ref[tile, side * ROWS : (side + 1) * ROWS] = shifted
                dot_ref[tile, side * ROWS : (side + 1) * ROWS] = dots
                total = total + jnp.sum(fold(shifted), axis=0)
                weighted = weighted + jnp.sum(fold(shifted * dots), axis=0)
            peak_ref[pl.ds(step, 1), :] = new_best
            return new_best, total, weighted

        empty = jnp.zeros((8, LANES), jnp.float32)
        sums = (jnp.full((1, LANES), MASKED_SCORE, jnp.float32), empty, empty)
        sums = lax.fori_loop(first, inner, functools.partial(scores_body, True), sums)
        sums = lax.fori_loop(inner, diagonal, functools.partial(scores_body, False), sums)
        best, total, weighted = lax.fori_loop(
            diagonal, last, functools.partial(scores_body, True), sums
        )
        share = 1.0 / jnp.sum(total, axis=0, keepdims=True)
        delta = jnp.sum(weighted, axis=0, keepdims=True) * share
        dqt_ref[...] = jnp.zeros_like(dqt_ref)

        def grads_body(step, carry):
            step_share = share * jnp.exp2(peak_ref[pl.ds(step, 1), :] - best)
            score_grads, norms_t = [], []
            for pair in range(PAIRS):
                tile = step * PAIRS + pair
                chance = chance_ref[tile] * step_share
                score_grad = (chance * (dot_ref[tile] - delta)).astype(jnp.bfloat16)
                dv_ref[tile] += nn_dot(chance.astype(jnp.bfloat16), grad)
                dk_ref[tile] += nn_dot(score_grad, query)
                score_grads.append(score_grad)
                norms_t += [held_turned[0, tile], held_turned[1, tile]]
            dqt_ref[...] += nn_dot(
                jnp.concatenate(norms_t, axis=1), jnp.concatenate(score_grads, axis=0)
            )
            return carry

        lax.fori_loop(first, last, grads_body, 0)
        query_grad = dqt_ref[...].T * FACTOR
        held_dq[block] = unit_norm_backward(
            query_grad, unit_rows, inverse, gain_ref[...]
        ).astype(jnp.bfloat16)
        gain_grad_ref[...] += jnp.sum(query_grad * unit_rows, axis=0, keepdims=True)
        return carry

    lax.fori_loop(0, DEPTH, block_body, 0)
    cast_ref[:, 0] = dv_ref[:, ROWS:].astype(jnp.bfloat16)
    cast_ref[:, 1] = dk_ref[:, ROWS:].astype(jnp.bfloat16)
    moves = [
        (held_dq, dq_ref),
        (cast_ref, other_ref),
        (dv_ref.at[:, :ROWS], own_ref.at[0]),
        (dk_ref.at[:, :ROWS], own_ref.at[1]),
    ]
    copies = [
        pltpu.make_async_copy(source, target, out_sem.at[index])
        for index, (source, target) in enumerate(moves)
    ]
    for copy in copies:
        copy.start()
    for copy in copies:
        copy.wait()


def attention(bounds, half, pos, low, gain, queries_grads, keys, raws):
    tiles = DEPTH
    pairs = DEPTH * tiles * ROWS * 2 * ROWS
    wide = pltpu.VMEM((tiles, 2 * ROWS, LANES), jnp.float32)
    total = pltpu.VMEM((tiles, 2 * ROWS, HD), jnp.float32)
    rows = pltpu.VMEM((tiles, ROWS, HD), jnp.bfloat16)
    outs = [
        jax.ShapeDtypeStruct((DEPTH, ROWS, HD), jnp.bfloat16),
        jax.ShapeDtypeStruct((1, HD), jnp.float32),
        jax.ShapeDtypeStruct((2, DEPTH, ROWS, HD), jnp.float32),
        jax.ShapeDtypeStruct((DEPTH, 2, ROWS, HD), jnp.bfloat16),
    ]
    return pl.pallas_call(
        attention_kernel,
        in_specs=[SMEM_SPEC, SMEM_SPEC, VMEM_SPEC, VMEM_SPEC, VMEM_SPEC] + [ANY_SPEC] * 7,
        out_specs=[ANY_SPEC, VMEM_SPEC, ANY_SPEC, ANY_SPEC],
        out_shape=outs,
        scratch_shapes=[
            wide, wide, pltpu.VMEM((tiles, LANES), jnp.float32), total, total,
            pltpu.VMEM((HD, LANES), jnp.float32),
            pltpu.VMEM((2, tiles, ROWS, HD), jnp.bfloat16),
            pltpu.VMEM((2, tiles, HD, ROWS), jnp.bfloat16),
            pltpu.VMEM((2, tiles, ROWS, HD), jnp.bfloat16),
            pltpu.VMEM((DEPTH, 2, ROWS, HD), jnp.bfloat16),
            rows, pltpu.VMEM((DEPTH, 2, ROWS, HD), jnp.bfloat16),
            pltpu.SemaphoreType.DMA((7,)),
            pltpu.SemaphoreType.DMA((4,)),
        ],
        compiler_params=pltpu.CompilerParams(vmem_limit_bytes=VMEM_LIMIT),
        cost_estimate=pl.CostEstimate(
            flops=12 * pairs * HD, bytes_accessed=2**23, transcendentals=pairs
        ),
        name="attention",
    )(
        bounds, half, pos, low, gain, queries_grads,
        *[key[0] for key in keys], *[key[1] for key in keys], *raws,
    )


def key_gain_kernel(own_ref, other_ref, raw_own, raw_other, out_ref):
    total = jnp.zeros((ROWS, HD), jnp.float32)
    for tile in range(DEPTH):
        for grad, raw_ref in ((own_ref[0, tile], raw_own), (other_ref[tile, 0], raw_other)):
            total += grad.astype(jnp.float32) * unit_norm(raw_ref[tile, 0])[0]
    out_ref[...] = jnp.sum(total, axis=0, keepdims=True) * FACTOR


def keys_of_pair():
    return pl.BlockSpec((DEPTH, 1, ROWS, HD), lambda i: (0, 0, 0, 0))


def key_gain(own, other, raws):
    return pl.pallas_call(
        key_gain_kernel,
        grid=(1,),
        in_specs=[
            pl.BlockSpec((1, DEPTH, ROWS, HD), lambda i: (1, 0, 0, 0)),
            pl.BlockSpec((DEPTH, 1, ROWS, HD), lambda i: (0, 1, 0, 0)),
            keys_of_pair(),
            keys_of_pair(),
        ],
        out_specs=whole(1, HD),
        out_shape=jax.ShapeDtypeStruct((1, HD), jnp.float32),
        cost_estimate=pl.CostEstimate(flops=0, bytes_accessed=5 * 2**19, transcendentals=0),
        name="key_gain",
    )(own, other, *raws)


def finish_kernel(
    own_ref, other_ref, raw_ref, gain_ref, out_ref
):
    for tile in range(DEPTH):
        value_sum = own_ref[0, tile] + other_ref[tile, 0].astype(jnp.float32)
        out_ref[tile, :ROWS] = value_sum.astype(jnp.bfloat16)
        grad_norm = (own_ref[1, tile] + other_ref[tile, 1].astype(jnp.float32)) * FACTOR
        unit_rows, inverse = unit_norm(raw_ref[tile, 0])
        out_ref[tile, ROWS : 2 * ROWS] = unit_norm_backward(
            grad_norm, unit_rows, inverse, gain_ref[...]
        ).astype(jnp.bfloat16)


def finish(own, other, raw, gain):
    rows = 2 * ROWS
    return pl.pallas_call(
        finish_kernel,
        grid=(1,),
        in_specs=[whole(2, DEPTH, ROWS, HD), whole(DEPTH, 2, ROWS, HD)]
        + [keys_of_pair(), whole(1, HD)],
        out_specs=whole(DEPTH, rows, HD),
        out_shape=jax.ShapeDtypeStruct((DEPTH, rows, HD), jnp.bfloat16),
        cost_estimate=pl.CostEstimate(flops=0, bytes_accessed=2**23, transcendentals=0),
        name="finish",
    )(own, other, raw, gain)


def project_kernel(part_ref, rows_ref, weight_ref, *refs):
    outs, joined_ref = refs[:-1], refs[-1]
    width = outs[0].shape[1]
    for head in range(rows_ref.shape[0]):
        joined_ref[:, head * HD : (head + 1) * HD] = rows_ref[head]
    for step, out_ref in enumerate(outs):
        base = lax.rem(part_ref[0] + step, len(outs)) * width
        for start in range(0, width, LANES):
            rows = pl.ds(pl.multiple_of(base + start, LANES), LANES)
            out_ref[:, start : start + LANES] = nt_dot(
                joined_ref[...], weight_ref[rows, :]
            ).astype(jnp.bfloat16)


def project(part, weight, rows, parts):
    heads, count, _ = rows.shape
    model, inner = weight.shape
    return pl.pallas_call(
        project_kernel,
        in_specs=[SMEM_SPEC, VMEM_SPEC, VMEM_SPEC],
        out_specs=[VMEM_SPEC] * parts,
        out_shape=[jax.ShapeDtypeStruct((count, model // parts), jnp.bfloat16)] * parts,
        scratch_shapes=[pltpu.VMEM((count, inner), jnp.bfloat16)],
        compiler_params=pltpu.CompilerParams(vmem_limit_bytes=20 * 1024 * 1024),
        cost_estimate=pl.CostEstimate(
            flops=2 * count * model * inner, bytes_accessed=2 * model * inner, transcendentals=0
        ),
        name="project",
    )(part, rows, weight)


def along_z(pieces):
    return lax.all_to_all(pieces, "ctx", 0, 0, axis_index_groups=Z_GROUPS)


def swap_half(piece):
    return lax.ppermute(piece, "ctx", HALF_SWAP)


def sum_tp(parts):
    count = len(parts)
    total = parts[0].astype(jnp.float32)
    for step in range(1, count):
        pairs = [(index, (index + step) % count) for index in range(count)]
        total = total + lax.ppermute(parts[step], "tp", pairs).astype(jnp.float32)
    return total.astype(jnp.bfloat16)


def spread_gains(gains, z):
    moved = [
        lax.ppermute(gains, "dp", [(i, (i + step) % 4) for i in range(4)]) for step in (1, 2, 3)
    ]
    total = (gains + moved[1]) + (moved[0] + moved[2])
    mine = jnp.arange(HEADS_LOCAL, dtype=jnp.int32)[:, None, None] == z
    total = jnp.where(mine, total[None], 0.0)
    for distance in (1, 2, 4, 8):
        total = total + lax.ppermute(total, "ctx", [(i, i ^ distance) for i in range(16)])
    return total


def local(q_raw, k_raw, values, d_out, q_gain, k_gain, q_weight, doc_lengths):
    ctx = lax.axis_index("ctx")
    z = ctx // 2
    half = lax.rem(ctx, 2)
    lengths = doc_lengths[0]
    starts = jnp.cumsum(lengths) - lengths
    q_gain_row = lax.dynamic_slice_in_dim(q_gain, z, 1, 0)
    k_gain_row = lax.dynamic_slice_in_dim(k_gain, z, 1, 0)

    pos = (2 * jnp.arange(8, dtype=jnp.int32)[:, None] + half) * ROWS + jnp.arange(
        ROWS, dtype=jnp.int32
    )
    low = jnp.max(
        jnp.where(starts[None, None, :] <= pos[:, :, None], starts[None, None, :], 0), axis=2
    )
    wide = 2 * ROWS * PAIRS
    first = low[:, 0] // wide
    last = pos[:, -1] // wide + 1
    inner = jnp.clip((low[:, -1] + wide - 1) // wide, first, last)
    diagonal = jnp.clip(pos[:, 0] // wide, inner, last)
    bounds = jnp.stack([first, inner, diagonal, last], axis=1).astype(jnp.int32)

    own = along_z(pack(k_raw[0], values[0]))
    sent, own = lax.optimization_barrier((pack(q_raw[0], d_out[0]), own))
    queries_grads = along_z(sent)
    other = swap_half(own)
    (norm_own, turned_own), (norm_other, turned_other) = (
        key_prep(k_gain_row, own),
        key_prep(k_gain_row, other),
    )
    dq, query_gain_sum, sums, other_sums = attention(
        bounds,
        half.reshape(1),
        pos,
        low,
        q_gain_row,
        queries_grads,
        ((norm_own, turned_own), (norm_other, turned_other)),
        (own, other),
    )

    returned = along_z(dq)
    moved = swap_half(other_sums)
    key_gain_sum = key_gain(sums, other_sums, (own, other))
    gains = spread_gains(jnp.concatenate([query_gain_sum, key_gain_sum], axis=0), z)
    key_gain_sum, returned = lax.optimization_barrier((key_gain_sum, returned))
    parts = project(lax.axis_index("tp").reshape(1), q_weight, returned, 4)
    moved, *parts = lax.optimization_barrier((moved, *parts))
    input_grad = sum_tp(parts)
    pieces_back = along_z(finish(sums, moved, own, k_gain_row))
    value_grad, key_grad = unpack(pieces_back)
    return (input_grad[None], key_grad[None], value_grad[None], gains[:, 0], gains[:, 1])


def solution(mesh):
    return jax.shard_map(
        local,
        mesh=mesh,
        in_specs=(
            P("dp", "ctx", "tp"),
            P("dp", "ctx", "tp"),
            P("dp", "ctx", "tp"),
            P("dp", "ctx", "tp"),
            P("tp", None),
            P("tp", None),
            P(None, "tp"),
            P("dp", None),
        ),
        out_specs=(
            P("dp", "ctx", "tp"),
            P("dp", "ctx", "tp"),
            P("dp", "ctx", "tp"),
            P("tp", None),
            P("tp", None),
        ),
        check_vma=False,
    )
```

```python
import functools

import jax
import jax.numpy as jnp
from jax import lax
from jax.experimental import pallas as pl
from jax.experimental.pallas import tpu as pltpu
from jax.sharding import PartitionSpec as P

NORM_EPSILON = 1e-05
MASKED_SCORE = -1e30
LEAST_PEAK = -1e20
HEADS_LOCAL = 8
HD = 128
ROWS = 256
LANES = 256
PAIRS = 2
WIDE = 2 * PAIRS * ROWS
EXTRA = 16
FACTOR = HD ** (-0.5)
EXP2_FACTOR = FACTOR * 1.4426950408889634
VMEM_LIMIT = 60 * 1024 * 1024

DEPTH = 8
Z_GROUPS = [[2 * z + half for z in range(8)] for half in range(2)]
HALF_SWAP = [(index, index ^ 1) for index in range(16)]


def nt_dot(a, b):
    return lax.dot_general(a, b, (((1,), (1,)), ((), ())), preferred_element_type=jnp.float32)


def nn_dot(a, b):
    return lax.dot_general(a, b, (((1,), (0,)), ((), ())), preferred_element_type=jnp.float32)


def unit_norm(raw):
    widened = raw.astype(jnp.float32)
    centered = widened - jnp.mean(widened, axis=1, keepdims=True)
    inverse = lax.rsqrt(jnp.mean(centered * centered, axis=1, keepdims=True) + NORM_EPSILON)
    return centered * inverse, inverse


def unit_norm_backward(grad_norm, unit_rows, inverse, gain):
    scaled = grad_norm * gain
    mean_grad = jnp.mean(scaled, axis=1, keepdims=True)
    mean_cross = jnp.mean(scaled * unit_rows, axis=1, keepdims=True)
    return (scaled - mean_grad - unit_rows * mean_cross) * inverse


VMEM_SPEC = pl.BlockSpec(memory_space=pltpu.VMEM)
SMEM_SPEC = pl.BlockSpec(memory_space=pltpu.SMEM)
ANY_SPEC = pl.BlockSpec(memory_space=pltpu.HBM)


def pack_kernel(first_ref, second_ref, out_ref, held_ref, in_sem, out_sem):
    def inward(head, which):
        return pltpu.make_async_copy(
            (first_ref, second_ref)[which].at[:, head * HD : (head + 1) * HD],
            held_ref.at[head, which],
            in_sem.at[head, which],
        )

    def outward(head):
        return pltpu.make_async_copy(held_ref.at[head], out_ref.at[head], out_sem.at[head])

    for head in range(HEADS_LOCAL):
        for which in range(2):
            inward(head, which).start()
    for head in range(HEADS_LOCAL):
        for which in range(2):
            inward(head, which).wait()
        outward(head).start()
    for head in range(HEADS_LOCAL):
        outward(head).wait()


def pack(first, second):
    shape = (HEADS_LOCAL, 2, ROWS, HD)
    return pl.pallas_call(
        pack_kernel,
        in_specs=[ANY_SPEC, ANY_SPEC],
        out_specs=ANY_SPEC,
        out_shape=jax.ShapeDtypeStruct(shape, jnp.bfloat16),
        scratch_shapes=[
            pltpu.VMEM(shape, jnp.bfloat16),
            pltpu.SemaphoreType.DMA((HEADS_LOCAL, 2)),
            pltpu.SemaphoreType.DMA((HEADS_LOCAL,)),
        ],
        cost_estimate=pl.CostEstimate(flops=0, bytes_accessed=2**22, transcendentals=0),
        name="pack",
    )(first, second)


def unpack_kernel(pieces_ref, *refs):
    outs, (held_ref, in_sem, out_sem) = refs[:2], refs[2:]

    def inward(head):
        return pltpu.make_async_copy(pieces_ref.at[head], held_ref.at[head], in_sem.at[head])

    def outward(head, which):
        return pltpu.make_async_copy(
            held_ref.at[head, which * ROWS : (which + 1) * ROWS],
            outs[which].at[:, head * HD : (head + 1) * HD],
            out_sem.at[head, which],
        )

    for head in range(HEADS_LOCAL):
        inward(head).start()
    for head in range(HEADS_LOCAL):
        inward(head).wait()
        for which in range(2):
            outward(head, which).start()
    for head in range(HEADS_LOCAL):
        for which in range(2):
            outward(head, which).wait()


def unpack(pieces):
    rows = jax.ShapeDtypeStruct((ROWS, HEADS_LOCAL * HD), jnp.bfloat16)
    return pl.pallas_call(
        unpack_kernel,
        in_specs=[ANY_SPEC],
        out_specs=[ANY_SPEC, ANY_SPEC],
        out_shape=[rows, rows],
        scratch_shapes=[
            pltpu.VMEM(pieces.shape, jnp.bfloat16),
            pltpu.SemaphoreType.DMA((HEADS_LOCAL,)),
            pltpu.SemaphoreType.DMA((HEADS_LOCAL, 2)),
        ],
        cost_estimate=pl.CostEstimate(flops=0, bytes_accessed=2**22, transcendentals=0),
        name="unpack",
    )(pieces)


def whole(*shape):
    return pl.BlockSpec(shape, lambda i: (0,) * len(shape))


def key_prep_kernel(gain_ref, raw_ref, norm_ref, turned_ref, held_raw, held_norm, held_turned, in_sem, out_sem):
    inward = [
        pltpu.make_async_copy(raw_ref.at[tile, 0], held_raw.at[tile], in_sem.at[tile])
        for tile in range(DEPTH)
    ]
    outward = [
        pltpu.make_async_copy(held_norm, norm_ref, out_sem.at[0]),
        pltpu.make_async_copy(held_turned, turned_ref, out_sem.at[1]),
    ]
    for copy in inward:
        copy.start()
    for tile in range(DEPTH):
        inward[tile].wait()
        unit_rows, _ = unit_norm(held_raw[tile])
        scaled = unit_rows * gain_ref[...]
        held_norm[tile] = scaled.astype(jnp.bfloat16)
        held_turned[tile] = scaled.T.astype(jnp.bfloat16)
    for copy in outward:
        copy.start()
    for copy in outward:
        copy.wait()


def key_prep(gain, keys_values):
    shapes = [(DEPTH, ROWS, HD), (DEPTH, HD, ROWS)]
    return pl.pallas_call(
        key_prep_kernel,
        in_specs=[VMEM_SPEC, ANY_SPEC],
        out_specs=[ANY_SPEC] * 2,
        out_shape=[jax.ShapeDtypeStruct(shape, jnp.bfloat16) for shape in shapes],
        scratch_shapes=[
            pltpu.VMEM(shapes[0], jnp.bfloat16),
            pltpu.VMEM(shapes[0], jnp.bfloat16),
            pltpu.VMEM(shapes[1], jnp.bfloat16),
            pltpu.SemaphoreType.DMA((DEPTH,)),
            pltpu.SemaphoreType.DMA((2,)),
        ],
        cost_estimate=pl.CostEstimate(flops=0, bytes_accessed=2**22, transcendentals=0),
        name="key_prep",
    )(gain, keys_values)


def fold(tile):
    return tile.reshape(tile.shape[0] // 8, 8, tile.shape[1])


def attention_kernel(bounds_ref, half_ref, pos_ref, low_ref, gain_ref, key_gain_ref, *refs):
    queries_grads_ref, refs = refs[0], refs[1:]
    norms, turned, raws = refs[0:2], refs[2:4], refs[4:6]
    refs = refs[6:]
    dq_ref, own_ref, other_ref = refs[:3]
    (
        chance_ref,
        dot_ref,
        peak_ref,
        dk_ref,
        dv_ref,
        dqt_ref,
        held_norm,
        held_turned,
        held_value,
        held_query,
        held_dq,
        cast_ref,
        gain_grad_ref,
        in_sem,
        dq_sem,
        out_sem,
    ) = refs[3:]
    half = half_ref[0]

    def loads(step):
        tiles = pl.ds(step * PAIRS, PAIRS)
        moves = [(queries_grads_ref.at[tiles], held_query.at[tiles])]
        for side in range(2):
            lanes = pl.ds(side * ROWS, ROWS)
            moves.append((norms[side].at[tiles], held_norm.at[tiles, side]))
            moves.append((turned[side].at[tiles], held_turned.at[tiles, :, lanes]))
            moves.append((raws[side].at[tiles, 1], held_value.at[tiles, side]))
        return [
            pltpu.make_async_copy(source, target, in_sem.at[step, index])
            for index, (source, target) in enumerate(moves)
        ]

    for step in range(DEPTH // PAIRS):
        for copy in loads(step):
            copy.start()
    dk_ref[...] = jnp.zeros_like(dk_ref)
    dv_ref[...] = jnp.zeros_like(dv_ref)
    gain_grad_ref[...] = jnp.zeros_like(gain_grad_ref)

    def block_body(block, carry):
        @pl.when(lax.rem(block, PAIRS) == 0)
        def _():
            for copy in loads(block // PAIRS):
                copy.wait()

        unit_rows, inverse = unit_norm(held_query[block, 0])
        query = (unit_rows * gain_ref[...]).astype(jnp.bfloat16)
        grad = held_query[block, 1]
        pos = pos_ref[pl.ds(block, 1), :]
        low = low_ref[pl.ds(block, 1), :]
        row = lax.broadcasted_iota(jnp.int32, (ROWS, LANES), 0)
        first, inner, diagonal, last = (bounds_ref[block, i] for i in range(4))

        def scores_body(masked, step, sums):
            best, total, weighted = sums
            parts = []
            peak = jnp.full((8, LANES), MASKED_SCORE, jnp.float32)
            for pair in range(PAIRS):
                tile = step * PAIRS + pair
                for side in range(2):
                    scores = nt_dot(held_norm[tile, side], query)
                    if masked:
                        which = half if side == 0 else 1 - half
                        base = (2 * tile + which) * ROWS
                        mask = row >= low - base
                        if masked > 1:
                            mask = mask & (row <= pos - base)
                        scores = jnp.where(mask, scores, MASKED_SCORE)
                    parts.append((tile, side, scores))
                    peak = jnp.maximum(peak, jnp.max(fold(scores), axis=0))
            new_best = jnp.maximum(best, jnp.max(peak, axis=0, keepdims=True) * EXP2_FACTOR)
            scale = jnp.exp2(best - new_best)
            total, weighted = total * scale, weighted * scale
            for index, (tile, side, scores) in enumerate(parts):
                shifted = jnp.exp2(scores * EXP2_FACTOR - new_best)
                dots = nt_dot(held_value[tile, side], grad)
                rows = slice(index * ROWS, (index + 1) * ROWS)
                chance_ref[step, rows] = shifted
                dot_ref[step, rows] = dots
                total = total + jnp.sum(fold(shifted), axis=0)
                weighted = weighted + jnp.sum(fold(shifted * dots), axis=0)
            peak_ref[pl.ds(step, 1), :] = new_best
            return new_best, total, weighted

        empty = jnp.zeros((8, LANES), jnp.float32)
        sums = (jnp.full((1, LANES), LEAST_PEAK, jnp.float32), empty, empty)
        sums = lax.fori_loop(first, inner, functools.partial(scores_body, 1), sums)
        sums = lax.fori_loop(inner, diagonal, functools.partial(scores_body, 0), sums)
        best, total, weighted = lax.fori_loop(
            diagonal, last, functools.partial(scores_body, 2), sums
        )
        share = 1.0 / jnp.sum(total, axis=0, keepdims=True)
        delta = jnp.sum(weighted, axis=0, keepdims=True) * share
        dqt_ref[...] = jnp.zeros_like(dqt_ref)

        def grads_body(step, carry):
            step_share = share * jnp.exp2(peak_ref[pl.ds(step, 1), :] - best)
            score_grads, keys_t = [], []
            for pair in range(PAIRS):
                rows = slice(pair * 2 * ROWS, (pair + 1) * 2 * ROWS)
                chance = chance_ref[step, rows] * step_share
                score_grad = (chance * (dot_ref[step, rows] - delta)).astype(jnp.bfloat16)
                dv_ref[step, rows] += nn_dot(chance.astype(jnp.bfloat16), grad)
                dk_ref[step, rows] += nn_dot(score_grad, query)
                score_grads.append(score_grad)
                keys_t.append(held_turned[step * PAIRS + pair])
            dqt_ref[...] += nn_dot(jnp.concatenate(keys_t, axis=1), jnp.concatenate(score_grads, axis=0))
            return carry

        lax.fori_loop(first, last, grads_body, 0)
        query_grad = dqt_ref[...].T * FACTOR
        held_dq[block, :ROWS] = unit_norm_backward(
            query_grad, unit_rows, inverse, gain_ref[...]
        ).astype(jnp.bfloat16)
        gain_grad_ref[...] += jnp.sum(query_grad * unit_rows, axis=0, keepdims=True)
        return carry

    lax.fori_loop(0, DEPTH, block_body, 0)
    key_total = jnp.zeros((ROWS, HD), jnp.float32)
    for tile in range(DEPTH):
        for side in range(2):
            start = (tile % PAIRS * 2 + side) * ROWS
            key_grad = dk_ref[tile // PAIRS, start : start + ROWS]
            key_total += key_grad * held_norm[tile, side].astype(jnp.float32)
    key_total = jnp.sum(key_total, axis=0, keepdims=True) * FACTOR / key_gain_ref[...]
    row = lax.broadcasted_iota(jnp.int32, (EXTRA, HD), 0)
    extra = jnp.zeros((EXTRA, HD), jnp.float32)
    for which, rest in enumerate((gain_grad_ref[...], key_total)):
        for index in range(3):
            term = rest.astype(jnp.bfloat16).astype(jnp.float32)
            extra = jnp.where(row == 3 * which + index, term, extra)
            rest = rest - term
    for tile in range(DEPTH):
        held_dq[tile, ROWS:] = extra.astype(jnp.bfloat16)
    copies = [pltpu.make_async_copy(held_dq, dq_ref, dq_sem.at[0])]
    copies[0].start()
    for tile in range(DEPTH):
        step, base = tile // PAIRS, tile % PAIRS * 2 * ROWS
        for side, out_ref in enumerate((own_ref, other_ref)):
            rows = slice(base + side * ROWS, base + (side + 1) * ROWS)
            cast_ref[side, tile, 0] = dv_ref[step, rows].astype(jnp.bfloat16)
            cast_ref[side, tile, 1] = dk_ref[step, rows].astype(jnp.bfloat16)
            copies.append(
                pltpu.make_async_copy(
                    cast_ref.at[side, tile], out_ref.at[tile], out_sem.at[side, tile]
                )
            )
            copies[-1].start()
    for copy in copies:
        copy.wait()


def attention(bounds, half, pos, low, gain, key_gain, queries_grads, keys, raws):
    steps = DEPTH // PAIRS
    pairs = DEPTH * DEPTH * ROWS * 2 * ROWS
    scores = pltpu.VMEM((steps, WIDE, LANES), jnp.float32)
    total = pltpu.VMEM((steps, WIDE, HD), jnp.float32)
    both = pltpu.VMEM((DEPTH, 2, ROWS, HD), jnp.bfloat16)
    sums = jax.ShapeDtypeStruct((DEPTH, 2, ROWS, HD), jnp.bfloat16)
    return pl.pallas_call(
        attention_kernel,
        in_specs=[SMEM_SPEC, SMEM_SPEC] + [VMEM_SPEC] * 4 + [ANY_SPEC] * 7,
        out_specs=[ANY_SPEC, ANY_SPEC, ANY_SPEC],
        out_shape=[
            jax.ShapeDtypeStruct((DEPTH, ROWS + EXTRA, HD), jnp.bfloat16),
            sums,
            sums,
        ],
        scratch_shapes=[
            scores, scores, pltpu.VMEM((DEPTH, LANES), jnp.float32), total, total,
            pltpu.VMEM((HD, LANES), jnp.float32),
            both,
            pltpu.VMEM((DEPTH, HD, 2 * ROWS), jnp.bfloat16),
            both,
            both,
            pltpu.VMEM((DEPTH, ROWS + EXTRA, HD), jnp.bfloat16),
            pltpu.VMEM((2, DEPTH, 2, ROWS, HD), jnp.bfloat16),
            pltpu.VMEM((1, HD), jnp.float32),
            pltpu.SemaphoreType.DMA((steps, 7)),
            pltpu.SemaphoreType.DMA((1,)),
            pltpu.SemaphoreType.DMA((2, DEPTH)),
        ],
        compiler_params=pltpu.CompilerParams(vmem_limit_bytes=VMEM_LIMIT),
        cost_estimate=pl.CostEstimate(
            flops=12 * pairs * HD, bytes_accessed=2**23, transcendentals=pairs
        ),
        name="attention",
    )(
        bounds, half, pos, low, gain, key_gain, queries_grads,
        *[key[0] for key in keys], *[key[1] for key in keys], *raws,
    )


def keys_of_pair():
    return pl.BlockSpec((DEPTH, 1, ROWS, HD), lambda i: (0, 0, 0, 0))


def finish_kernel(
    own_ref, other_ref, raw_ref, gain_ref, out_ref
):
    for tile in range(DEPTH):
        value_sum = own_ref[tile, 0].astype(jnp.float32) + other_ref[tile, 0].astype(jnp.float32)
        out_ref[tile, :ROWS] = value_sum.astype(jnp.bfloat16)
        grad_norm = own_ref[tile, 1].astype(jnp.float32) + other_ref[tile, 1].astype(jnp.float32)
        grad_norm = grad_norm * FACTOR
        unit_rows, inverse = unit_norm(raw_ref[tile, 0])
        out_ref[tile, ROWS : 2 * ROWS] = unit_norm_backward(
            grad_norm, unit_rows, inverse, gain_ref[...]
        ).astype(jnp.bfloat16)


def finish(own, other, raw, gain):
    rows = 2 * ROWS
    return pl.pallas_call(
        finish_kernel,
        grid=(1,),
        in_specs=[whole(DEPTH, 2, ROWS, HD), whole(DEPTH, 2, ROWS, HD)]
        + [keys_of_pair(), whole(1, HD)],
        out_specs=whole(DEPTH, rows, HD),
        out_shape=jax.ShapeDtypeStruct((DEPTH, rows, HD), jnp.bfloat16),
        cost_estimate=pl.CostEstimate(flops=0, bytes_accessed=2**23, transcendentals=0),
        compiler_params=pltpu.CompilerParams(vmem_limit_bytes=16 * 1024 * 1024),
        name="finish",
    )(own, other, raw, gain)


def project_kernel(part_ref, rows_ref, weight_ref, *refs):
    outs, (gains_ref, joined_ref) = refs[:-2], refs[-2:]
    width = outs[0].shape[1]
    for head in range(rows_ref.shape[0]):
        joined_ref[:, head * HD : (head + 1) * HD] = rows_ref[head, :ROWS]
        terms = rows_ref[head, ROWS:].astype(jnp.float32)
        for which in range(2):
            first, second, third = (terms[3 * which + i : 3 * which + i + 1] for i in range(3))
            place = which * HEADS_LOCAL + head
            gains_ref[place : place + 1, :] = (third + second) + first
    for step, out_ref in enumerate(outs):
        base = lax.rem(part_ref[0] + step, len(outs)) * width
        for start in range(0, width, LANES):
            rows = pl.ds(pl.multiple_of(base + start, LANES), LANES)
            out_ref[:, start : start + LANES] = nt_dot(
                joined_ref[...], weight_ref[rows, :]
            ).astype(jnp.bfloat16)


def project(part, weight, rows, parts):
    model, inner = weight.shape
    out = jax.ShapeDtypeStruct((ROWS, model // parts), jnp.bfloat16)
    return pl.pallas_call(
        project_kernel,
        in_specs=[SMEM_SPEC, VMEM_SPEC, VMEM_SPEC],
        out_specs=[VMEM_SPEC] * (parts + 1),
        out_shape=[out] * parts + [jax.ShapeDtypeStruct((2 * HEADS_LOCAL, HD), jnp.float32)],
        scratch_shapes=[pltpu.VMEM((ROWS, inner), jnp.bfloat16)],
        compiler_params=pltpu.CompilerParams(vmem_limit_bytes=20 * 1024 * 1024),
        cost_estimate=pl.CostEstimate(
            flops=2 * ROWS * model * inner, bytes_accessed=2 * model * inner, transcendentals=0
        ),
        name="project",
    )(part, rows, weight)


def along_z(pieces):
    return lax.all_to_all(pieces, "ctx", 0, 0, axis_index_groups=Z_GROUPS)


def swap_half(piece):
    return lax.ppermute(piece, "ctx", HALF_SWAP)


def sum_tp(parts):
    count = len(parts)
    total = parts[0].astype(jnp.float32)
    for step in range(1, count):
        pairs = [(index, (index + step) % count) for index in range(count)]
        total = total + lax.ppermute(parts[step], "tp", pairs).astype(jnp.float32)
    return total.astype(jnp.bfloat16)


def sum_gains(gains):
    moved = [
        lax.ppermute(gains, "dp", [(i, (i + step) % 4) for i in range(4)]) for step in (1, 2, 3)
    ]
    total = (gains + moved[1]) + (moved[0] + moved[2])
    return total + swap_half(total)


def local(q_raw, k_raw, values, d_out, q_gain, k_gain, q_weight, doc_lengths):
    ctx = lax.axis_index("ctx")
    z = ctx // 2
    half = lax.rem(ctx, 2)
    lengths = doc_lengths[0]
    starts = jnp.cumsum(lengths) - lengths
    q_gain_row = lax.dynamic_slice_in_dim(q_gain, z, 1, 0)
    k_gain_row = lax.dynamic_slice_in_dim(k_gain, z, 1, 0)

    pos = (2 * jnp.arange(8, dtype=jnp.int32)[:, None] + half) * ROWS + jnp.arange(
        ROWS, dtype=jnp.int32
    )
    low = jnp.max(
        jnp.where(starts[None, None, :] <= pos[:, :, None], starts[None, None, :], 0), axis=2
    )
    wide = 2 * ROWS * PAIRS
    first = low[:, 0] // wide
    last = pos[:, -1] // wide + 1
    diagonal = jnp.clip(pos[:, 0] // wide, first, last)
    inner = jnp.clip((low[:, -1] + wide - 1) // wide, first, diagonal)
    bounds = jnp.stack([first, inner, diagonal, last], axis=1).astype(jnp.int32)

    own = along_z(pack(k_raw[0], values[0]))
    sent, own = lax.optimization_barrier((pack(q_raw[0], d_out[0]), own))
    queries_grads = along_z(sent)
    other = swap_half(own)
    (norm_own, turned_own), (norm_other, turned_other) = (
        key_prep(k_gain_row, own),
        key_prep(k_gain_row, other),
    )
    dq, sums, other_sums = attention(
        bounds,
        half.reshape(1),
        pos,
        low,
        q_gain_row,
        k_gain_row,
        queries_grads,
        ((norm_own, turned_own), (norm_other, turned_other)),
        (own, other),
    )

    returned = along_z(dq)
    moved = swap_half(other_sums)
    *parts, gains = project(lax.axis_index("tp").reshape(1), q_weight, returned, 4)
    moved, *parts = lax.optimization_barrier((moved, *parts))
    input_grad = sum_tp(parts)
    finished = finish(sums, moved, own, k_gain_row)
    gains, finished = lax.optimization_barrier((gains, finished))
    gains = sum_gains(gains)
    value_grad, key_grad = unpack(along_z(finished))
    return (input_grad[None], key_grad[None], value_grad[None], gains[:HEADS_LOCAL], gains[HEADS_LOCAL:])


def solution(mesh):
    return jax.shard_map(
        local,
        mesh=mesh,
        in_specs=(
            P("dp", "ctx", "tp"),
            P("dp", "ctx", "tp"),
            P("dp", "ctx", "tp"),
            P("dp", "ctx", "tp"),
            P("tp", None),
            P("tp", None),
            P(None, "tp"),
            P("dp", None),
        ),
        out_specs=(
            P("dp", "ctx", "tp"),
            P("dp", "ctx", "tp"),
            P("dp", "ctx", "tp"),
            P("tp", None),
            P("tp", None),
        ),
        check_vma=False,
    )
```

```python
import functools

import jax
import jax.numpy as jnp
from jax import lax
from jax.experimental import pallas as pl
from jax.experimental.pallas import tpu as pltpu
from jax.sharding import PartitionSpec as P

NORM_EPSILON = 1e-05
MASKED_SCORE = -1e30
LEAST_PEAK = -1e20
HEADS_LOCAL = 8
HD = 128
ROWS = 256
LANES = 512
COLUMNS = 256
PAIRS = 2
WIDE = 2 * PAIRS * ROWS
EXTRA = 16
FACTOR = HD ** (-0.5)
EXP2_FACTOR = FACTOR * 1.4426950408889634
VMEM_LIMIT = 60 * 1024 * 1024

DEPTH = 8
Z_GROUPS = [[2 * z + half for z in range(8)] for half in range(2)]
HALF_SWAP = [(index, index ^ 1) for index in range(16)]


def nt_dot(a, b):
    return lax.dot_general(a, b, (((1,), (1,)), ((), ())), preferred_element_type=jnp.float32)


def nn_dot(a, b):
    return lax.dot_general(a, b, (((1,), (0,)), ((), ())), preferred_element_type=jnp.float32)


def unit_norm(raw):
    widened = raw.astype(jnp.float32)
    centered = widened - jnp.mean(widened, axis=1, keepdims=True)
    inverse = lax.rsqrt(jnp.mean(centered * centered, axis=1, keepdims=True) + NORM_EPSILON)
    return centered * inverse, inverse


def unit_norm_backward(grad_norm, unit_rows, inverse, gain):
    scaled = grad_norm * gain
    mean_grad = jnp.mean(scaled, axis=1, keepdims=True)
    mean_cross = jnp.mean(scaled * unit_rows, axis=1, keepdims=True)
    return (scaled - mean_grad - unit_rows * mean_cross) * inverse


VMEM_SPEC = pl.BlockSpec(memory_space=pltpu.VMEM)
SMEM_SPEC = pl.BlockSpec(memory_space=pltpu.SMEM)
ANY_SPEC = pl.BlockSpec(memory_space=pltpu.HBM)


def pack_kernel(first_ref, second_ref, out_ref, held_ref, in_sem, out_sem):
    def inward(head, which):
        return pltpu.make_async_copy(
            (first_ref, second_ref)[which].at[:, head * HD : (head + 1) * HD],
            held_ref.at[head, which],
            in_sem.at[head, which],
        )

    def outward(head):
        return pltpu.make_async_copy(held_ref.at[head], out_ref.at[head], out_sem.at[head])

    for head in range(HEADS_LOCAL):
        for which in range(2):
            inward(head, which).start()
    for head in range(HEADS_LOCAL):
        for which in range(2):
            inward(head, which).wait()
        outward(head).start()
    for head in range(HEADS_LOCAL):
        outward(head).wait()


def pack(first, second):
    shape = (HEADS_LOCAL, 2, ROWS, HD)
    return pl.pallas_call(
        pack_kernel,
        in_specs=[ANY_SPEC, ANY_SPEC],
        out_specs=ANY_SPEC,
        out_shape=jax.ShapeDtypeStruct(shape, jnp.bfloat16),
        scratch_shapes=[
            pltpu.VMEM(shape, jnp.bfloat16),
            pltpu.SemaphoreType.DMA((HEADS_LOCAL, 2)),
            pltpu.SemaphoreType.DMA((HEADS_LOCAL,)),
        ],
        cost_estimate=pl.CostEstimate(flops=0, bytes_accessed=2**22, transcendentals=0),
        name="pack",
    )(first, second)


def unpack_kernel(pieces_ref, *refs):
    outs, (held_ref, in_sem, out_sem) = refs[:2], refs[2:]

    def inward(head):
        return pltpu.make_async_copy(pieces_ref.at[head], held_ref.at[head], in_sem.at[head])

    def outward(head, which):
        return pltpu.make_async_copy(
            held_ref.at[head, which * ROWS : (which + 1) * ROWS],
            outs[which].at[:, head * HD : (head + 1) * HD],
            out_sem.at[head, which],
        )

    for head in range(HEADS_LOCAL):
        inward(head).start()
    for head in range(HEADS_LOCAL):
        inward(head).wait()
        for which in range(2):
            outward(head, which).start()
    for head in range(HEADS_LOCAL):
        for which in range(2):
            outward(head, which).wait()


def unpack(pieces):
    rows = jax.ShapeDtypeStruct((ROWS, HEADS_LOCAL * HD), jnp.bfloat16)
    return pl.pallas_call(
        unpack_kernel,
        in_specs=[pl.BlockSpec(memory_space=pl.ANY)],
        out_specs=[ANY_SPEC, ANY_SPEC],
        out_shape=[rows, rows],
        scratch_shapes=[
            pltpu.VMEM(pieces.shape, jnp.bfloat16),
            pltpu.SemaphoreType.DMA((HEADS_LOCAL,)),
            pltpu.SemaphoreType.DMA((HEADS_LOCAL, 2)),
        ],
        cost_estimate=pl.CostEstimate(flops=0, bytes_accessed=2**22, transcendentals=0),
        compiler_params=pltpu.CompilerParams(vmem_limit_bytes=16 * 1024 * 1024),
        name="unpack",
    )(pieces)


def whole(*shape):
    return pl.BlockSpec(shape, lambda i: (0,) * len(shape))


def key_prep_kernel(gain_ref, raw_ref, norm_ref, turned_ref, held_raw, held_norm, held_turned, in_sem, out_sem):
    inward = [
        pltpu.make_async_copy(raw_ref.at[tile, 0], held_raw.at[tile], in_sem.at[tile])
        for tile in range(DEPTH)
    ]
    outward = [
        pltpu.make_async_copy(held_norm, norm_ref, out_sem.at[0]),
        pltpu.make_async_copy(held_turned, turned_ref, out_sem.at[1]),
    ]
    for copy in inward:
        copy.start()
    for tile in range(DEPTH):
        inward[tile].wait()
        unit_rows, _ = unit_norm(held_raw[tile])
        scaled = unit_rows * gain_ref[...]
        held_norm[tile] = scaled.astype(jnp.bfloat16)
        held_turned[tile] = scaled.T.astype(jnp.bfloat16)
    for copy in outward:
        copy.start()
    for copy in outward:
        copy.wait()


def key_prep(gain, keys_values):
    shapes = [(DEPTH, ROWS, HD), (DEPTH, HD, ROWS)]
    return pl.pallas_call(
        key_prep_kernel,
        in_specs=[VMEM_SPEC, ANY_SPEC],
        out_specs=[ANY_SPEC] * 2,
        out_shape=[jax.ShapeDtypeStruct(shape, jnp.bfloat16) for shape in shapes],
        scratch_shapes=[
            pltpu.VMEM(shapes[0], jnp.bfloat16),
            pltpu.VMEM(shapes[0], jnp.bfloat16),
            pltpu.VMEM(shapes[1], jnp.bfloat16),
            pltpu.SemaphoreType.DMA((DEPTH,)),
            pltpu.SemaphoreType.DMA((2,)),
        ],
        cost_estimate=pl.CostEstimate(flops=0, bytes_accessed=2**22, transcendentals=0),
        name="key_prep",
    )(gain, keys_values)


def fold(tile):
    return tile.reshape(tile.shape[0] // 8, 8, tile.shape[1])


def attention_kernel(bounds_ref, half_ref, pos_ref, low_ref, gain_ref, key_gain_ref, *refs):
    queries_grads_ref, refs = refs[0], refs[1:]
    norms, turned, raws = refs[0:2], refs[2:4], refs[4:6]
    refs = refs[6:]
    dq_ref, own_ref, other_ref = refs[:3]
    (
        chance_ref,
        dot_ref,
        peak_ref,
        dk_ref,
        dv_ref,
        dqt_ref,
        held_norm,
        held_turned,
        held_value,
        held_query,
        held_dq,
        cast_ref,
        gain_grad_ref,
        in_sem,
        dq_sem,
        out_sem,
    ) = refs[3:]
    half = half_ref[0]

    def loads(step):
        tiles = pl.ds(step * PAIRS, PAIRS)
        moves = [(queries_grads_ref.at[tiles], held_query.at[tiles])]
        for side in range(2):
            lanes = pl.ds(side * ROWS, ROWS)
            moves.append((norms[side].at[tiles], held_norm.at[tiles, side]))
            moves.append((turned[side].at[tiles], held_turned.at[tiles, :, lanes]))
            moves.append((raws[side].at[tiles, 1], held_value.at[tiles, side]))
        return [
            pltpu.make_async_copy(source, target, in_sem.at[step, index])
            for index, (source, target) in enumerate(moves)
        ]

    for step in range(DEPTH // PAIRS):
        for copy in loads(step):
            copy.start()
    dk_ref[...] = jnp.zeros_like(dk_ref)
    dv_ref[...] = jnp.zeros_like(dv_ref)
    gain_grad_ref[...] = jnp.zeros_like(gain_grad_ref)

    def block_body(block, carry):
        for copy in loads(block):
            copy.wait()
        shards = [block * PAIRS + pair for pair in range(PAIRS)]
        unit_rows, inverse = unit_norm(
            jnp.concatenate([held_query[shard, 0] for shard in shards], axis=0)
        )
        query = (unit_rows * gain_ref[...]).astype(jnp.bfloat16)
        grad = jnp.concatenate([held_query[shard, 1] for shard in shards], axis=0)
        pos = pos_ref[pl.ds(block, 1), :]
        low = low_ref[pl.ds(block, 1), :]
        row = lax.broadcasted_iota(jnp.int32, (ROWS, LANES), 0)
        first, inner, diagonal, last = (bounds_ref[block, i] for i in range(4))

        def scores_body(masked, step, sums):
            best, total, weighted = sums
            parts = []
            peak = jnp.full((8, LANES), MASKED_SCORE, jnp.float32)
            for pair in range(PAIRS):
                tile = step * PAIRS + pair
                for side in range(2):
                    scores = nt_dot(held_norm[tile, side], query)
                    if masked:
                        which = half if side == 0 else 1 - half
                        base = (2 * tile + which) * ROWS
                        mask = row >= low - base
                        if masked > 1:
                            mask = mask & (row <= pos - base)
                        scores = jnp.where(mask, scores, MASKED_SCORE)
                    parts.append((tile, side, scores))
                    peak = jnp.maximum(peak, jnp.max(fold(scores), axis=0))
            new_best = jnp.maximum(best, jnp.max(peak, axis=0, keepdims=True) * EXP2_FACTOR)
            scale = jnp.exp2(best - new_best)
            total, weighted = total * scale, weighted * scale
            for index, (tile, side, scores) in enumerate(parts):
                shifted = jnp.exp2(scores * EXP2_FACTOR - new_best)
                dots = nt_dot(held_value[tile, side], grad)
                rows = slice(index * ROWS, (index + 1) * ROWS)
                chance_ref[step, rows] = shifted
                dot_ref[step, rows] = dots
                total = total + jnp.sum(fold(shifted), axis=0)
                weighted = weighted + jnp.sum(fold(shifted * dots), axis=0)
            peak_ref[pl.ds(step, 1), :] = new_best
            return new_best, total, weighted

        empty = jnp.zeros((8, LANES), jnp.float32)
        sums = (jnp.full((1, LANES), LEAST_PEAK, jnp.float32), empty, empty)
        sums = lax.fori_loop(first, inner, functools.partial(scores_body, 1), sums)
        sums = lax.fori_loop(inner, diagonal, functools.partial(scores_body, 0), sums)
        best, total, weighted = lax.fori_loop(
            diagonal, last, functools.partial(scores_body, 2), sums
        )
        share = 1.0 / jnp.sum(total, axis=0, keepdims=True)
        delta = jnp.sum(weighted, axis=0, keepdims=True) * share
        dqt_ref[...] = jnp.zeros_like(dqt_ref)

        def grads_body(step, carry):
            step_share = share * jnp.exp2(peak_ref[pl.ds(step, 1), :] - best)
            score_grads, keys_t = [], []
            for pair in range(PAIRS):
                rows = slice(pair * 2 * ROWS, (pair + 1) * 2 * ROWS)
                chance = chance_ref[step, rows] * step_share
                score_grad = (chance * (dot_ref[step, rows] - delta)).astype(jnp.bfloat16)
                dv_ref[step, rows] += nn_dot(chance.astype(jnp.bfloat16), grad)
                dk_ref[step, rows] += nn_dot(score_grad, query)
                score_grads.append(score_grad)
                keys_t.append(held_turned[step * PAIRS + pair])
            dqt_ref[...] += nn_dot(jnp.concatenate(keys_t, axis=1), jnp.concatenate(score_grads, axis=0))
            return carry

        lax.fori_loop(first, last, grads_body, 0)
        query_grad = dqt_ref[...].T * FACTOR
        raw_grad = unit_norm_backward(query_grad, unit_rows, inverse, gain_ref[...])
        for pair, shard in enumerate(shards):
            rows = slice(pair * ROWS, (pair + 1) * ROWS)
            held_dq[shard, :ROWS] = raw_grad[rows].astype(jnp.bfloat16)
        gain_grad_ref[...] += jnp.sum(query_grad * unit_rows, axis=0, keepdims=True)
        return carry

    lax.fori_loop(0, DEPTH // PAIRS, block_body, 0)
    key_total = jnp.zeros((ROWS, HD), jnp.float32)
    for tile in range(DEPTH):
        for side in range(2):
            start = (tile % PAIRS * 2 + side) * ROWS
            key_grad = dk_ref[tile // PAIRS, start : start + ROWS]
            key_total += key_grad * held_norm[tile, side].astype(jnp.float32)
    key_total = jnp.sum(key_total, axis=0, keepdims=True) * FACTOR / key_gain_ref[...]
    row = lax.broadcasted_iota(jnp.int32, (EXTRA, HD), 0)
    extra = jnp.zeros((EXTRA, HD), jnp.float32)
    for which, rest in enumerate((gain_grad_ref[...], key_total)):
        for index in range(3):
            term = rest.astype(jnp.bfloat16).astype(jnp.float32)
            extra = jnp.where(row == 3 * which + index, term, extra)
            rest = rest - term
    for tile in range(DEPTH):
        held_dq[tile, ROWS:] = extra.astype(jnp.bfloat16)
    copies = [pltpu.make_async_copy(held_dq, dq_ref, dq_sem.at[0])]
    copies[0].start()
    for tile in range(DEPTH):
        step, base = tile // PAIRS, tile % PAIRS * 2 * ROWS
        for side, out_ref in enumerate((own_ref, other_ref)):
            rows = slice(base + side * ROWS, base + (side + 1) * ROWS)
            cast_ref[side, tile, 0] = dv_ref[step, rows].astype(jnp.bfloat16)
            cast_ref[side, tile, 1] = dk_ref[step, rows].astype(jnp.bfloat16)
            copies.append(
                pltpu.make_async_copy(
                    cast_ref.at[side, tile], out_ref.at[tile], out_sem.at[side, tile]
                )
            )
            copies[-1].start()
    for copy in copies:
        copy.wait()


def attention(bounds, half, pos, low, gain, key_gain, queries_grads, keys, raws):
    steps = DEPTH // PAIRS
    pairs = DEPTH * DEPTH * ROWS * 2 * ROWS
    scores = pltpu.VMEM((steps, WIDE, LANES), jnp.float32)
    total = pltpu.VMEM((steps, WIDE, HD), jnp.float32)
    both = pltpu.VMEM((DEPTH, 2, ROWS, HD), jnp.bfloat16)
    sums = jax.ShapeDtypeStruct((DEPTH, 2, ROWS, HD), jnp.bfloat16)
    return pl.pallas_call(
        attention_kernel,
        in_specs=[SMEM_SPEC, SMEM_SPEC] + [VMEM_SPEC] * 4 + [ANY_SPEC] * 7,
        out_specs=[ANY_SPEC, ANY_SPEC, ANY_SPEC],
        out_shape=[
            jax.ShapeDtypeStruct((DEPTH, ROWS + EXTRA, HD), jnp.bfloat16),
            sums,
            sums,
        ],
        scratch_shapes=[
            scores, scores, pltpu.VMEM((DEPTH, LANES), jnp.float32), total, total,
            pltpu.VMEM((HD, LANES), jnp.float32),
            both,
            pltpu.VMEM((DEPTH, HD, 2 * ROWS), jnp.bfloat16),
            both,
            both,
            pltpu.VMEM((DEPTH, ROWS + EXTRA, HD), jnp.bfloat16),
            pltpu.VMEM((2, DEPTH, 2, ROWS, HD), jnp.bfloat16),
            pltpu.VMEM((1, HD), jnp.float32),
            pltpu.SemaphoreType.DMA((steps, 7)),
            pltpu.SemaphoreType.DMA((1,)),
            pltpu.SemaphoreType.DMA((2, DEPTH)),
        ],
        compiler_params=pltpu.CompilerParams(vmem_limit_bytes=VMEM_LIMIT),
        cost_estimate=pl.CostEstimate(
            flops=12 * pairs * HD, bytes_accessed=2**23, transcendentals=pairs
        ),
        name="attention",
    )(
        bounds, half, pos, low, gain, key_gain, queries_grads,
        *[key[0] for key in keys], *[key[1] for key in keys], *raws,
    )


def keys_of_pair():
    return pl.BlockSpec((DEPTH, 1, ROWS, HD), lambda i: (0, 0, 0, 0))


def finish_kernel(
    own_ref, other_ref, raw_ref, gain_ref, out_ref
):
    for tile in range(DEPTH):
        value_sum = own_ref[tile, 0].astype(jnp.float32) + other_ref[tile, 0].astype(jnp.float32)
        out_ref[tile, :ROWS] = value_sum.astype(jnp.bfloat16)
        grad_norm = own_ref[tile, 1].astype(jnp.float32) + other_ref[tile, 1].astype(jnp.float32)
        grad_norm = grad_norm * FACTOR
        unit_rows, inverse = unit_norm(raw_ref[tile, 0])
        out_ref[tile, ROWS : 2 * ROWS] = unit_norm_backward(
            grad_norm, unit_rows, inverse, gain_ref[...]
        ).astype(jnp.bfloat16)


def finish(own, other, raw, gain):
    rows = 2 * ROWS
    return pl.pallas_call(
        finish_kernel,
        grid=(1,),
        in_specs=[whole(DEPTH, 2, ROWS, HD), whole(DEPTH, 2, ROWS, HD)]
        + [keys_of_pair(), whole(1, HD)],
        out_specs=whole(DEPTH, rows, HD),
        out_shape=jax.ShapeDtypeStruct((DEPTH, rows, HD), jnp.bfloat16),
        cost_estimate=pl.CostEstimate(flops=0, bytes_accessed=2**23, transcendentals=0),
        compiler_params=pltpu.CompilerParams(vmem_limit_bytes=16 * 1024 * 1024),
        name="finish",
    )(own, other, raw, gain)


def project_kernel(part_ref, rows_ref, weight_ref, *refs):
    outs, (gains_ref, joined_ref) = refs[:-2], refs[-2:]
    width = outs[0].shape[1]
    for head in range(rows_ref.shape[0]):
        joined_ref[:, head * HD : (head + 1) * HD] = rows_ref[head, :ROWS]
        terms = rows_ref[head, ROWS:].astype(jnp.float32)
        for which in range(2):
            first, second, third = (terms[3 * which + i : 3 * which + i + 1] for i in range(3))
            place = which * HEADS_LOCAL + head
            gains_ref[place : place + 1, :] = (third + second) + first
    for step, out_ref in enumerate(outs):
        base = lax.rem(part_ref[0] + step, len(outs)) * width
        for start in range(0, width, COLUMNS):
            rows = pl.ds(pl.multiple_of(base + start, COLUMNS), COLUMNS)
            out_ref[:, start : start + COLUMNS] = nt_dot(
                joined_ref[...], weight_ref[rows, :]
            ).astype(jnp.bfloat16)


def project(part, weight, rows, parts):
    model, inner = weight.shape
    out = jax.ShapeDtypeStruct((ROWS, model // parts), jnp.bfloat16)
    return pl.pallas_call(
        project_kernel,
        in_specs=[SMEM_SPEC, VMEM_SPEC, VMEM_SPEC],
        out_specs=[VMEM_SPEC] * (parts + 1),
        out_shape=[out] * parts + [jax.ShapeDtypeStruct((2 * HEADS_LOCAL, HD), jnp.float32)],
        scratch_shapes=[pltpu.VMEM((ROWS, inner), jnp.bfloat16)],
        compiler_params=pltpu.CompilerParams(vmem_limit_bytes=20 * 1024 * 1024),
        cost_estimate=pl.CostEstimate(
            flops=2 * ROWS * model * inner, bytes_accessed=2 * model * inner, transcendentals=0
        ),
        name="project",
    )(part, rows, weight)


def along_z(pieces):
    return lax.all_to_all(pieces, "ctx", 0, 0, axis_index_groups=Z_GROUPS)


def swap_half(piece):
    return lax.ppermute(piece, "ctx", HALF_SWAP)


def sum_tp(parts):
    count = len(parts)
    total = parts[0].astype(jnp.float32)
    for step in range(1, count):
        pairs = [(index, (index + step) % count) for index in range(count)]
        total = total + lax.ppermute(parts[step], "tp", pairs).astype(jnp.float32)
    return total.astype(jnp.bfloat16)


def sum_gains(gains):
    moved = [
        lax.ppermute(gains, "dp", [(i, (i + step) % 4) for i in range(4)]) for step in (1, 2, 3)
    ]
    total = (gains + moved[1]) + (moved[0] + moved[2])
    return total + swap_half(total)


def local(q_raw, k_raw, values, d_out, q_gain, k_gain, q_weight, doc_lengths):
    ctx = lax.axis_index("ctx")
    z = ctx // 2
    half = lax.rem(ctx, 2)
    lengths = doc_lengths[0]
    starts = jnp.cumsum(lengths) - lengths
    q_gain_row = lax.dynamic_slice_in_dim(q_gain, z, 1, 0)
    k_gain_row = lax.dynamic_slice_in_dim(k_gain, z, 1, 0)

    pos = (2 * jnp.arange(8, dtype=jnp.int32)[:, None] + half) * ROWS + jnp.arange(
        ROWS, dtype=jnp.int32
    )
    pos = pos.reshape(DEPTH // PAIRS, LANES)
    low = jnp.max(
        jnp.where(starts[None, None, :] <= pos[:, :, None], starts[None, None, :], 0), axis=2
    )
    wide = 2 * ROWS * PAIRS
    first = low[:, 0] // wide
    last = pos[:, -1] // wide + 1
    diagonal = jnp.clip(pos[:, 0] // wide, first, last)
    inner = jnp.clip((low[:, -1] + wide - 1) // wide, first, diagonal)
    bounds = jnp.stack([first, inner, diagonal, last], axis=1).astype(jnp.int32)

    own = along_z(pack(k_raw[0], values[0]))
    sent, own = lax.optimization_barrier((pack(q_raw[0], d_out[0]), own))
    queries_grads = along_z(sent)
    other = swap_half(own)
    (norm_own, turned_own), (norm_other, turned_other) = (
        key_prep(k_gain_row, own),
        key_prep(k_gain_row, other),
    )
    dq, sums, other_sums = attention(
        bounds,
        half.reshape(1),
        pos,
        low,
        q_gain_row,
        k_gain_row,
        queries_grads,
        ((norm_own, turned_own), (norm_other, turned_other)),
        (own, other),
    )

    returned = along_z(dq)
    moved = swap_half(other_sums)
    *parts, gains = project(lax.axis_index("tp").reshape(1), q_weight, returned, 4)
    moved, *parts = lax.optimization_barrier((moved, *parts))
    input_grad = sum_tp(parts)
    finished = finish(sums, moved, own, k_gain_row)
    gains, finished = lax.optimization_barrier((gains, finished))
    gains = sum_gains(gains)
    value_grad, key_grad = unpack(along_z(finished))
    return (input_grad[None], key_grad[None], value_grad[None], gains[:HEADS_LOCAL], gains[HEADS_LOCAL:])


def solution(mesh):
    return jax.shard_map(
        local,
        mesh=mesh,
        in_specs=(
            P("dp", "ctx", "tp"),
            P("dp", "ctx", "tp"),
            P("dp", "ctx", "tp"),
            P("dp", "ctx", "tp"),
            P("tp", None),
            P("tp", None),
            P(None, "tp"),
            P("dp", None),
        ),
        out_specs=(
            P("dp", "ctx", "tp"),
            P("dp", "ctx", "tp"),
            P("dp", "ctx", "tp"),
            P("tp", None),
            P("tp", None),
        ),
        check_vma=False,
    )
```

```python
import functools

import jax
import jax.numpy as jnp
from jax import lax
from jax.experimental import pallas as pl
from jax.experimental.pallas import tpu as pltpu
from jax.sharding import PartitionSpec as P

NORM_EPSILON = 1e-05
MASKED_SCORE = -1e30
LEAST_PEAK = -1e20
HEADS_LOCAL = 8
HD = 128
ROWS = 256
LANES = 512
COLUMNS = 256
PAIRS = 2
WIDE = 2 * PAIRS * ROWS
EXTRA = 16
FACTOR = HD ** (-0.5)
EXP2_FACTOR = FACTOR * 1.4426950408889634
VMEM_LIMIT = 60 * 1024 * 1024

DEPTH = 8
Z_GROUPS = [[2 * z + half for z in range(8)] for half in range(2)]
HALF_SWAP = [(index, index ^ 1) for index in range(16)]


def nt_dot(a, b):
    return lax.dot_general(a, b, (((1,), (1,)), ((), ())), preferred_element_type=jnp.float32)


def nn_dot(a, b):
    return lax.dot_general(a, b, (((1,), (0,)), ((), ())), preferred_element_type=jnp.float32)


def unit_norm(raw):
    widened = raw.astype(jnp.float32)
    centered = widened - jnp.mean(widened, axis=1, keepdims=True)
    inverse = lax.rsqrt(jnp.mean(centered * centered, axis=1, keepdims=True) + NORM_EPSILON)
    return centered * inverse, inverse


def unit_norm_backward(grad_norm, unit_rows, inverse, gain):
    scaled = grad_norm * gain
    mean_grad = jnp.mean(scaled, axis=1, keepdims=True)
    mean_cross = jnp.mean(scaled * unit_rows, axis=1, keepdims=True)
    return (scaled - mean_grad - unit_rows * mean_cross) * inverse


VMEM_SPEC = pl.BlockSpec(memory_space=pltpu.VMEM)
SMEM_SPEC = pl.BlockSpec(memory_space=pltpu.SMEM)
ANY_SPEC = pl.BlockSpec(memory_space=pltpu.HBM)


def pack_kernel(first_ref, second_ref, out_ref, held_ref, in_sem, out_sem):
    def inward(head, which):
        return pltpu.make_async_copy(
            (first_ref, second_ref)[which].at[:, head * HD : (head + 1) * HD],
            held_ref.at[head, which],
            in_sem.at[head, which],
        )

    def outward(head):
        return pltpu.make_async_copy(held_ref.at[head], out_ref.at[head], out_sem.at[head])

    for head in range(HEADS_LOCAL):
        for which in range(2):
            inward(head, which).start()
    for head in range(HEADS_LOCAL):
        for which in range(2):
            inward(head, which).wait()
        outward(head).start()
    for head in range(HEADS_LOCAL):
        outward(head).wait()


def pack(first, second):
    shape = (HEADS_LOCAL, 2, ROWS, HD)
    return pl.pallas_call(
        pack_kernel,
        in_specs=[ANY_SPEC, ANY_SPEC],
        out_specs=ANY_SPEC,
        out_shape=jax.ShapeDtypeStruct(shape, jnp.bfloat16),
        scratch_shapes=[
            pltpu.VMEM(shape, jnp.bfloat16),
            pltpu.SemaphoreType.DMA((HEADS_LOCAL, 2)),
            pltpu.SemaphoreType.DMA((HEADS_LOCAL,)),
        ],
        cost_estimate=pl.CostEstimate(flops=0, bytes_accessed=2**22, transcendentals=0),
        name="pack",
    )(first, second)


def unpack_kernel(pieces_ref, *refs):
    outs, (held_ref, in_sem, out_sem) = refs[:2], refs[2:]

    def inward(head):
        return pltpu.make_async_copy(pieces_ref.at[head], held_ref.at[head], in_sem.at[head])

    def outward(head, which):
        return pltpu.make_async_copy(
            held_ref.at[head, which * ROWS : (which + 1) * ROWS],
            outs[which].at[:, head * HD : (head + 1) * HD],
            out_sem.at[head, which],
        )

    for head in range(HEADS_LOCAL):
        inward(head).start()
    for head in range(HEADS_LOCAL):
        inward(head).wait()
        for which in range(2):
            outward(head, which).start()
    for head in range(HEADS_LOCAL):
        for which in range(2):
            outward(head, which).wait()


def unpack(pieces):
    rows = jax.ShapeDtypeStruct((ROWS, HEADS_LOCAL * HD), jnp.bfloat16)
    return pl.pallas_call(
        unpack_kernel,
        in_specs=[pl.BlockSpec(memory_space=pl.ANY)],
        out_specs=[ANY_SPEC, ANY_SPEC],
        out_shape=[rows, rows],
        scratch_shapes=[
            pltpu.VMEM(pieces.shape, jnp.bfloat16),
            pltpu.SemaphoreType.DMA((HEADS_LOCAL,)),
            pltpu.SemaphoreType.DMA((HEADS_LOCAL, 2)),
        ],
        cost_estimate=pl.CostEstimate(flops=0, bytes_accessed=2**22, transcendentals=0),
        compiler_params=pltpu.CompilerParams(vmem_limit_bytes=16 * 1024 * 1024),
        name="unpack",
    )(pieces)


def whole(*shape):
    return pl.BlockSpec(shape, lambda i: (0,) * len(shape))


def key_prep_kernel(paired, gain_ref, raw_ref, norm_ref, turned_ref, held_raw, held_norm, held_turned, in_sem, out_sem):
    inward = [
        pltpu.make_async_copy(
            raw_ref.at[tile, 0] if paired else raw_ref.at[tile],
            held_raw.at[tile],
            in_sem.at[tile],
        )
        for tile in range(DEPTH)
    ]
    outward = [
        pltpu.make_async_copy(held_norm, norm_ref, out_sem.at[0]),
        pltpu.make_async_copy(held_turned, turned_ref, out_sem.at[1]),
    ]
    for copy in inward:
        copy.start()
    for tile in range(DEPTH):
        inward[tile].wait()
        unit_rows, _ = unit_norm(held_raw[tile])
        scaled = unit_rows * gain_ref[...]
        held_norm[tile] = scaled.astype(jnp.bfloat16)
        held_turned[tile] = scaled.T.astype(jnp.bfloat16)
    for copy in outward:
        copy.start()
    for copy in outward:
        copy.wait()


def key_prep(gain, keys):
    paired = keys.ndim == 4
    shapes = [(DEPTH, ROWS, HD), (DEPTH, HD, ROWS)]
    return pl.pallas_call(
        functools.partial(key_prep_kernel, paired),
        in_specs=[VMEM_SPEC, ANY_SPEC],
        out_specs=[ANY_SPEC] * 2,
        out_shape=[jax.ShapeDtypeStruct(shape, jnp.bfloat16) for shape in shapes],
        scratch_shapes=[
            pltpu.VMEM(shapes[0], jnp.bfloat16),
            pltpu.VMEM(shapes[0], jnp.bfloat16),
            pltpu.VMEM(shapes[1], jnp.bfloat16),
            pltpu.SemaphoreType.DMA((DEPTH,)),
            pltpu.SemaphoreType.DMA((2,)),
        ],
        cost_estimate=pl.CostEstimate(flops=0, bytes_accessed=2**22, transcendentals=0),
        name="key_prep",
    )(gain, keys)


def fold(tile):
    return tile.reshape(tile.shape[0] // 8, 8, tile.shape[1])


def attention_kernel(bounds_ref, half_ref, pos_ref, low_ref, gain_ref, key_gain_ref, *refs):
    queries_grads_ref, refs = refs[0], refs[1:]
    norms, turned, raws = refs[0:2], refs[2:4], refs[4:6]
    refs = refs[6:]
    dq_ref, own_ref, other_ref = refs[:3]
    (
        chance_ref,
        dot_ref,
        peak_ref,
        dk_ref,
        dv_ref,
        dqt_ref,
        held_norm,
        held_turned,
        held_value,
        held_query,
        held_dq,
        cast_ref,
        gain_grad_ref,
        in_sem,
        dq_sem,
        out_sem,
    ) = refs[3:]
    half = half_ref[0]

    def loads(step):
        tiles = pl.ds(step * PAIRS, PAIRS)
        moves = [(queries_grads_ref.at[tiles], held_query.at[tiles])]
        for side in range(2):
            lanes = pl.ds(side * ROWS, ROWS)
            moves.append((norms[side].at[tiles], held_norm.at[tiles, side]))
            moves.append((turned[side].at[tiles], held_turned.at[tiles, :, lanes]))
            value = raws[0].at[tiles, 1] if side == 0 else raws[1].at[tiles]
            moves.append((value, held_value.at[tiles, side]))
        return [
            pltpu.make_async_copy(source, target, in_sem.at[step, index])
            for index, (source, target) in enumerate(moves)
        ]

    for step in range(DEPTH // PAIRS):
        for copy in loads(step):
            copy.start()
    dk_ref[...] = jnp.zeros_like(dk_ref)
    dv_ref[...] = jnp.zeros_like(dv_ref)
    gain_grad_ref[...] = jnp.zeros_like(gain_grad_ref)

    def block_body(block, carry):
        for copy in loads(block):
            copy.wait()
        shards = [block * PAIRS + pair for pair in range(PAIRS)]
        unit_rows, inverse = unit_norm(
            jnp.concatenate([held_query[shard, 0] for shard in shards], axis=0)
        )
        query = (unit_rows * gain_ref[...]).astype(jnp.bfloat16)
        grad = jnp.concatenate([held_query[shard, 1] for shard in shards], axis=0)
        pos = pos_ref[pl.ds(block, 1), :]
        low = low_ref[pl.ds(block, 1), :]
        row = lax.broadcasted_iota(jnp.int32, (ROWS, LANES), 0)
        first, inner, diagonal, last = (bounds_ref[block, i] for i in range(4))

        def scores_body(masked, step, sums):
            best, total, weighted = sums
            parts = []
            peak = jnp.full((8, LANES), MASKED_SCORE, jnp.float32)
            for pair in range(PAIRS):
                tile = step * PAIRS + pair
                for side in range(2):
                    scores = nt_dot(held_norm[tile, side], query)
                    if masked:
                        which = half if side == 0 else 1 - half
                        base = (2 * tile + which) * ROWS
                        mask = row >= low - base
                        if masked > 1:
                            mask = mask & (row <= pos - base)
                        scores = jnp.where(mask, scores, MASKED_SCORE)
                    parts.append((tile, side, scores))
                    peak = jnp.maximum(peak, jnp.max(fold(scores), axis=0))
            new_best = jnp.maximum(best, jnp.max(peak, axis=0, keepdims=True) * EXP2_FACTOR)
            scale = jnp.exp2(best - new_best)
            total, weighted = total * scale, weighted * scale
            for index, (tile, side, scores) in enumerate(parts):
                shifted = jnp.exp2(scores * EXP2_FACTOR - new_best)
                dots = nt_dot(held_value[tile, side], grad)
                rows = slice(index * ROWS, (index + 1) * ROWS)
                chance_ref[step, rows] = shifted
                dot_ref[step, rows] = dots
                total = total + jnp.sum(fold(shifted), axis=0)
                weighted = weighted + jnp.sum(fold(shifted * dots), axis=0)
            peak_ref[pl.ds(step, 1), :] = new_best
            return new_best, total, weighted

        empty = jnp.zeros((8, LANES), jnp.float32)
        sums = (jnp.full((1, LANES), LEAST_PEAK, jnp.float32), empty, empty)
        sums = lax.fori_loop(first, inner, functools.partial(scores_body, 1), sums)
        sums = lax.fori_loop(inner, diagonal, functools.partial(scores_body, 0), sums)
        best, total, weighted = lax.fori_loop(
            diagonal, last, functools.partial(scores_body, 2), sums
        )
        share = 1.0 / jnp.sum(total, axis=0, keepdims=True)
        delta = jnp.sum(weighted, axis=0, keepdims=True) * share
        dqt_ref[...] = jnp.zeros_like(dqt_ref)

        def grads_body(step, carry):
            step_share = share * jnp.exp2(peak_ref[pl.ds(step, 1), :] - best)
            score_grads, keys_t = [], []
            for pair in range(PAIRS):
                rows = slice(pair * 2 * ROWS, (pair + 1) * 2 * ROWS)
                chance = chance_ref[step, rows] * step_share
                score_grad = (chance * (dot_ref[step, rows] - delta)).astype(jnp.bfloat16)
                dv_ref[step, rows] += nn_dot(chance.astype(jnp.bfloat16), grad)
                dk_ref[step, rows] += nn_dot(score_grad, query)
                score_grads.append(score_grad)
                keys_t.append(held_turned[step * PAIRS + pair])
            dqt_ref[...] += nn_dot(jnp.concatenate(keys_t, axis=1), jnp.concatenate(score_grads, axis=0))
            return carry

        lax.fori_loop(first, last, grads_body, 0)
        query_grad = dqt_ref[...].T * FACTOR
        raw_grad = unit_norm_backward(query_grad, unit_rows, inverse, gain_ref[...])
        for pair, shard in enumerate(shards):
            rows = slice(pair * ROWS, (pair + 1) * ROWS)
            held_dq[shard, :ROWS] = raw_grad[rows].astype(jnp.bfloat16)
        gain_grad_ref[...] += jnp.sum(query_grad * unit_rows, axis=0, keepdims=True)
        return carry

    lax.fori_loop(0, DEPTH // PAIRS, block_body, 0)
    key_total = jnp.zeros((ROWS, HD), jnp.float32)
    for tile in range(DEPTH):
        for side in range(2):
            start = (tile % PAIRS * 2 + side) * ROWS
            key_grad = dk_ref[tile // PAIRS, start : start + ROWS]
            key_total += key_grad * held_norm[tile, side].astype(jnp.float32)
    key_total = jnp.sum(key_total, axis=0, keepdims=True) * FACTOR / key_gain_ref[...]
    row = lax.broadcasted_iota(jnp.int32, (EXTRA, HD), 0)
    extra = jnp.zeros((EXTRA, HD), jnp.float32)
    for which, rest in enumerate((gain_grad_ref[...], key_total)):
        for index in range(3):
            term = rest.astype(jnp.bfloat16).astype(jnp.float32)
            extra = jnp.where(row == 3 * which + index, term, extra)
            rest = rest - term
    for tile in range(DEPTH):
        held_dq[tile, ROWS:] = extra.astype(jnp.bfloat16)
    copies = [pltpu.make_async_copy(held_dq, dq_ref, dq_sem.at[0])]
    copies[0].start()
    for tile in range(DEPTH):
        step, base = tile // PAIRS, tile % PAIRS * 2 * ROWS
        for side, out_ref in enumerate((own_ref, other_ref)):
            rows = slice(base + side * ROWS, base + (side + 1) * ROWS)
            cast_ref[side, tile, 0] = dv_ref[step, rows].astype(jnp.bfloat16)
            cast_ref[side, tile, 1] = dk_ref[step, rows].astype(jnp.bfloat16)
            copies.append(
                pltpu.make_async_copy(
                    cast_ref.at[side, tile], out_ref.at[tile], out_sem.at[side, tile]
                )
            )
            copies[-1].start()
    for copy in copies:
        copy.wait()


def attention(bounds, half, pos, low, gain, key_gain, queries_grads, keys, raws):
    steps = DEPTH // PAIRS
    pairs = DEPTH * DEPTH * ROWS * 2 * ROWS
    scores = pltpu.VMEM((steps, WIDE, LANES), jnp.float32)
    total = pltpu.VMEM((steps, WIDE, HD), jnp.float32)
    both = pltpu.VMEM((DEPTH, 2, ROWS, HD), jnp.bfloat16)
    sums = jax.ShapeDtypeStruct((DEPTH, 2, ROWS, HD), jnp.bfloat16)
    return pl.pallas_call(
        attention_kernel,
        in_specs=[SMEM_SPEC, SMEM_SPEC] + [VMEM_SPEC] * 4 + [ANY_SPEC] * 7,
        out_specs=[ANY_SPEC, ANY_SPEC, ANY_SPEC],
        out_shape=[
            jax.ShapeDtypeStruct((DEPTH, ROWS + EXTRA, HD), jnp.bfloat16),
            sums,
            sums,
        ],
        scratch_shapes=[
            scores, scores, pltpu.VMEM((DEPTH, LANES), jnp.float32), total, total,
            pltpu.VMEM((HD, LANES), jnp.float32),
            both,
            pltpu.VMEM((DEPTH, HD, 2 * ROWS), jnp.bfloat16),
            both,
            both,
            pltpu.VMEM((DEPTH, ROWS + EXTRA, HD), jnp.bfloat16),
            pltpu.VMEM((2, DEPTH, 2, ROWS, HD), jnp.bfloat16),
            pltpu.VMEM((1, HD), jnp.float32),
            pltpu.SemaphoreType.DMA((steps, 7)),
            pltpu.SemaphoreType.DMA((1,)),
            pltpu.SemaphoreType.DMA((2, DEPTH)),
        ],
        compiler_params=pltpu.CompilerParams(vmem_limit_bytes=VMEM_LIMIT),
        cost_estimate=pl.CostEstimate(
            flops=12 * pairs * HD, bytes_accessed=2**23, transcendentals=pairs
        ),
        name="attention",
    )(
        bounds, half, pos, low, gain, key_gain, queries_grads,
        *[key[0] for key in keys], *[key[1] for key in keys], *raws,
    )


def keys_of_pair():
    return pl.BlockSpec((DEPTH, 1, ROWS, HD), lambda i: (0, 0, 0, 0))


def finish_kernel(
    own_ref, other_ref, raw_ref, gain_ref, out_ref
):
    for tile in range(DEPTH):
        value_sum = own_ref[tile, 0].astype(jnp.float32) + other_ref[tile, 0].astype(jnp.float32)
        out_ref[tile, :ROWS] = value_sum.astype(jnp.bfloat16)
        grad_norm = own_ref[tile, 1].astype(jnp.float32) + other_ref[tile, 1].astype(jnp.float32)
        grad_norm = grad_norm * FACTOR
        unit_rows, inverse = unit_norm(raw_ref[tile, 0])
        out_ref[tile, ROWS : 2 * ROWS] = unit_norm_backward(
            grad_norm, unit_rows, inverse, gain_ref[...]
        ).astype(jnp.bfloat16)


def finish(own, other, raw, gain):
    rows = 2 * ROWS
    return pl.pallas_call(
        finish_kernel,
        grid=(1,),
        in_specs=[whole(DEPTH, 2, ROWS, HD), whole(DEPTH, 2, ROWS, HD)]
        + [keys_of_pair(), whole(1, HD)],
        out_specs=whole(DEPTH, rows, HD),
        out_shape=jax.ShapeDtypeStruct((DEPTH, rows, HD), jnp.bfloat16),
        cost_estimate=pl.CostEstimate(flops=0, bytes_accessed=2**23, transcendentals=0),
        compiler_params=pltpu.CompilerParams(vmem_limit_bytes=16 * 1024 * 1024),
        name="finish",
    )(own, other, raw, gain)


def project_kernel(part_ref, rows_ref, weight_ref, *refs):
    outs, (gains_ref, joined_ref) = refs[:-2], refs[-2:]
    width = outs[0].shape[1]
    for head in range(rows_ref.shape[0]):
        joined_ref[:, head * HD : (head + 1) * HD] = rows_ref[head, :ROWS]
        terms = rows_ref[head, ROWS:].astype(jnp.float32)
        for which in range(2):
            first, second, third = (terms[3 * which + i : 3 * which + i + 1] for i in range(3))
            place = which * HEADS_LOCAL + head
            gains_ref[place : place + 1, :] = (third + second) + first
    for step, out_ref in enumerate(outs):
        base = lax.rem(part_ref[0] + step, len(outs)) * width
        for start in range(0, width, COLUMNS):
            rows = pl.ds(pl.multiple_of(base + start, COLUMNS), COLUMNS)
            out_ref[:, start : start + COLUMNS] = nt_dot(
                joined_ref[...], weight_ref[rows, :]
            ).astype(jnp.bfloat16)


def project(part, weight, rows, parts):
    model, inner = weight.shape
    out = jax.ShapeDtypeStruct((ROWS, model // parts), jnp.bfloat16)
    return pl.pallas_call(
        project_kernel,
        in_specs=[SMEM_SPEC, VMEM_SPEC, VMEM_SPEC],
        out_specs=[VMEM_SPEC] * (parts + 1),
        out_shape=[out] * parts + [jax.ShapeDtypeStruct((2 * HEADS_LOCAL, HD), jnp.float32)],
        scratch_shapes=[pltpu.VMEM((ROWS, inner), jnp.bfloat16)],
        compiler_params=pltpu.CompilerParams(vmem_limit_bytes=20 * 1024 * 1024),
        cost_estimate=pl.CostEstimate(
            flops=2 * ROWS * model * inner, bytes_accessed=2 * model * inner, transcendentals=0
        ),
        name="project",
    )(part, rows, weight)


def along_z(pieces):
    return lax.all_to_all(pieces, "ctx", 0, 0, axis_index_groups=Z_GROUPS)


def swap_half(piece):
    return lax.ppermute(piece, "ctx", HALF_SWAP)


def sum_tp(parts):
    count = len(parts)
    total = parts[0].astype(jnp.float32)
    for step in range(1, count):
        pairs = [(index, (index + step) % count) for index in range(count)]
        total = total + lax.ppermute(parts[step], "tp", pairs).astype(jnp.float32)
    return total.astype(jnp.bfloat16)


def sum_gains(gains):
    moved = [
        lax.ppermute(gains, "dp", [(i, (i + step) % 4) for i in range(4)]) for step in (1, 2, 3)
    ]
    total = (gains + moved[1]) + (moved[0] + moved[2])
    return total + swap_half(total)


def local(q_raw, k_raw, values, d_out, q_gain, k_gain, q_weight, doc_lengths):
    ctx = lax.axis_index("ctx")
    z = ctx // 2
    half = lax.rem(ctx, 2)
    lengths = doc_lengths[0]
    starts = jnp.cumsum(lengths) - lengths
    q_gain_row = lax.dynamic_slice_in_dim(q_gain, z, 1, 0)
    k_gain_row = lax.dynamic_slice_in_dim(k_gain, z, 1, 0)

    pos = (2 * jnp.arange(8, dtype=jnp.int32)[:, None] + half) * ROWS + jnp.arange(
        ROWS, dtype=jnp.int32
    )
    pos = pos.reshape(DEPTH // PAIRS, LANES)
    low = jnp.max(
        jnp.where(starts[None, None, :] <= pos[:, :, None], starts[None, None, :], 0), axis=2
    )
    wide = 2 * ROWS * PAIRS
    first = low[:, 0] // wide
    last = pos[:, -1] // wide + 1
    diagonal = jnp.clip(pos[:, 0] // wide, first, last)
    inner = jnp.clip((low[:, -1] + wide - 1) // wide, first, diagonal)
    bounds = jnp.stack([first, inner, diagonal, last], axis=1).astype(jnp.int32)

    own = along_z(pack(k_raw[0], values[0]))
    sent, own = lax.optimization_barrier((pack(q_raw[0], d_out[0]), own))
    queries_grads = along_z(sent)
    key_other = swap_half(own[:, 0])
    keys_own = key_prep(k_gain_row, own)
    value_own, key_other, *keys_own = lax.optimization_barrier(
        (own[:, 1], key_other, *keys_own)
    )
    value_other = swap_half(value_own)
    (norm_own, turned_own), (norm_other, turned_other) = (
        keys_own,
        key_prep(k_gain_row, key_other),
    )
    dq, sums, other_sums = attention(
        bounds,
        half.reshape(1),
        pos,
        low,
        q_gain_row,
        k_gain_row,
        queries_grads,
        ((norm_own, turned_own), (norm_other, turned_other)),
        (own, value_other),
    )

    returned = along_z(dq)
    moved = swap_half(other_sums)
    *parts, gains = project(lax.axis_index("tp").reshape(1), q_weight, returned, 4)
    moved, *parts = lax.optimization_barrier((moved, *parts))
    input_grad = sum_tp(parts)
    finished = finish(sums, moved, own, k_gain_row)
    gains, finished = lax.optimization_barrier((gains, finished))
    gains = sum_gains(gains)
    value_grad, key_grad = unpack(along_z(finished))
    return (input_grad[None], key_grad[None], value_grad[None], gains[:HEADS_LOCAL], gains[HEADS_LOCAL:])


def solution(mesh):
    return jax.shard_map(
        local,
        mesh=mesh,
        in_specs=(
            P("dp", "ctx", "tp"),
            P("dp", "ctx", "tp"),
            P("dp", "ctx", "tp"),
            P("dp", "ctx", "tp"),
            P("tp", None),
            P("tp", None),
            P(None, "tp"),
            P("dp", None),
        ),
        out_specs=(
            P("dp", "ctx", "tp"),
            P("dp", "ctx", "tp"),
            P("dp", "ctx", "tp"),
            P("tp", None),
            P("tp", None),
        ),
        check_vma=False,
    )
```

```python
import functools

import jax
import jax.numpy as jnp
from jax import lax
from jax.experimental import pallas as pl
from jax.experimental.pallas import tpu as pltpu
from jax.sharding import PartitionSpec as P

NORM_EPSILON = 1e-05
MASKED_SCORE = -1e30
LEAST_PEAK = -1e20
HEADS_LOCAL = 8
HD = 128
ROWS = 256
LANES = 512
COLUMNS = 256
PAIRS = 2
WIDE = 2 * PAIRS * ROWS
EXTRA = 16
FACTOR = HD ** (-0.5)
EXP2_FACTOR = FACTOR * 1.4426950408889634
VMEM_LIMIT = 60 * 1024 * 1024

DEPTH = 8
Z_GROUPS = [[2 * z + half for z in range(8)] for half in range(2)]
HALF_SWAP = [(index, index ^ 1) for index in range(16)]


def nt_dot(a, b):
    return lax.dot_general(a, b, (((1,), (1,)), ((), ())), preferred_element_type=jnp.float32)


def nn_dot(a, b):
    return lax.dot_general(a, b, (((1,), (0,)), ((), ())), preferred_element_type=jnp.float32)


def unit_norm(raw):
    widened = raw.astype(jnp.float32)
    centered = widened - jnp.mean(widened, axis=1, keepdims=True)
    inverse = lax.rsqrt(jnp.mean(centered * centered, axis=1, keepdims=True) + NORM_EPSILON)
    return centered * inverse, inverse


def unit_norm_backward(grad_norm, unit_rows, inverse, gain):
    scaled = grad_norm * gain
    mean_grad = jnp.mean(scaled, axis=1, keepdims=True)
    mean_cross = jnp.mean(scaled * unit_rows, axis=1, keepdims=True)
    return (scaled - mean_grad - unit_rows * mean_cross) * inverse


VMEM_SPEC = pl.BlockSpec(memory_space=pltpu.VMEM)
SMEM_SPEC = pl.BlockSpec(memory_space=pltpu.SMEM)
ANY_SPEC = pl.BlockSpec(memory_space=pltpu.HBM)


def pack_kernel(first_ref, second_ref, out_ref, held_ref, in_sem, out_sem):
    def inward(head, which):
        return pltpu.make_async_copy(
            (first_ref, second_ref)[which].at[:, head * HD : (head + 1) * HD],
            held_ref.at[head, which],
            in_sem.at[head, which],
        )

    def outward(head):
        return pltpu.make_async_copy(held_ref.at[head], out_ref.at[head], out_sem.at[head])

    for head in range(HEADS_LOCAL):
        for which in range(2):
            inward(head, which).start()
    for head in range(HEADS_LOCAL):
        for which in range(2):
            inward(head, which).wait()
        outward(head).start()
    for head in range(HEADS_LOCAL):
        outward(head).wait()


def pack(first, second):
    shape = (HEADS_LOCAL, 2, ROWS, HD)
    return pl.pallas_call(
        pack_kernel,
        in_specs=[ANY_SPEC, ANY_SPEC],
        out_specs=ANY_SPEC,
        out_shape=jax.ShapeDtypeStruct(shape, jnp.bfloat16),
        scratch_shapes=[
            pltpu.VMEM(shape, jnp.bfloat16),
            pltpu.SemaphoreType.DMA((HEADS_LOCAL, 2)),
            pltpu.SemaphoreType.DMA((HEADS_LOCAL,)),
        ],
        cost_estimate=pl.CostEstimate(flops=0, bytes_accessed=2**22, transcendentals=0),
        name="pack",
    )(first, second)


def unpack_kernel(pieces_ref, *refs):
    outs, (held_ref, in_sem, out_sem) = refs[:2], refs[2:]

    def inward(head):
        return pltpu.make_async_copy(pieces_ref.at[head], held_ref.at[head], in_sem.at[head])

    def outward(head, which):
        return pltpu.make_async_copy(
            held_ref.at[head, which * ROWS : (which + 1) * ROWS],
            outs[which].at[:, head * HD : (head + 1) * HD],
            out_sem.at[head, which],
        )

    for head in range(HEADS_LOCAL):
        inward(head).start()
    for head in range(HEADS_LOCAL):
        inward(head).wait()
        for which in range(2):
            outward(head, which).start()
    for head in range(HEADS_LOCAL):
        for which in range(2):
            outward(head, which).wait()


def unpack(pieces):
    rows = jax.ShapeDtypeStruct((ROWS, HEADS_LOCAL * HD), jnp.bfloat16)
    return pl.pallas_call(
        unpack_kernel,
        in_specs=[pl.BlockSpec(memory_space=pl.ANY)],
        out_specs=[ANY_SPEC, ANY_SPEC],
        out_shape=[rows, rows],
        scratch_shapes=[
            pltpu.VMEM(pieces.shape, jnp.bfloat16),
            pltpu.SemaphoreType.DMA((HEADS_LOCAL,)),
            pltpu.SemaphoreType.DMA((HEADS_LOCAL, 2)),
        ],
        cost_estimate=pl.CostEstimate(flops=0, bytes_accessed=2**22, transcendentals=0),
        compiler_params=pltpu.CompilerParams(vmem_limit_bytes=16 * 1024 * 1024),
        name="unpack",
    )(pieces)


def whole(*shape):
    return pl.BlockSpec(shape, lambda i: (0,) * len(shape))


def key_prep_kernel(paired, gain_ref, raw_ref, norm_ref, turned_ref, held_raw, held_norm, held_turned, in_sem, out_sem):
    inward = [
        pltpu.make_async_copy(
            raw_ref.at[tile, 0] if paired else raw_ref.at[tile],
            held_raw.at[tile],
            in_sem.at[tile],
        )
        for tile in range(DEPTH)
    ]
    outward = [
        pltpu.make_async_copy(held_norm, norm_ref, out_sem.at[0]),
        pltpu.make_async_copy(held_turned, turned_ref, out_sem.at[1]),
    ]
    for copy in inward:
        copy.start()
    for tile in range(DEPTH):
        inward[tile].wait()
        unit_rows, _ = unit_norm(held_raw[tile])
        scaled = unit_rows * gain_ref[...]
        held_norm[tile] = scaled.astype(jnp.bfloat16)
        held_turned[tile] = scaled.T.astype(jnp.bfloat16)
    for copy in outward:
        copy.start()
    for copy in outward:
        copy.wait()


def key_prep(gain, keys):
    paired = keys.ndim == 4
    shapes = [(DEPTH, ROWS, HD), (DEPTH, HD, ROWS)]
    return pl.pallas_call(
        functools.partial(key_prep_kernel, paired),
        in_specs=[VMEM_SPEC, ANY_SPEC],
        out_specs=[ANY_SPEC] * 2,
        out_shape=[jax.ShapeDtypeStruct(shape, jnp.bfloat16) for shape in shapes],
        scratch_shapes=[
            pltpu.VMEM(shapes[0], jnp.bfloat16),
            pltpu.VMEM(shapes[0], jnp.bfloat16),
            pltpu.VMEM(shapes[1], jnp.bfloat16),
            pltpu.SemaphoreType.DMA((DEPTH,)),
            pltpu.SemaphoreType.DMA((2,)),
        ],
        cost_estimate=pl.CostEstimate(flops=0, bytes_accessed=2**22, transcendentals=0),
        name="key_prep",
    )(gain, keys)


def fold(tile):
    return tile.reshape(tile.shape[0] // 8, 8, tile.shape[1])


def attention_kernel(bounds_ref, half_ref, pos_ref, low_ref, gain_ref, key_gain_ref, *refs):
    queries_grads_ref, refs = refs[0], refs[1:]
    norms, turned, raws = refs[0:2], refs[2:4], refs[4:6]
    refs = refs[6:]
    dq_ref, own_ref, other_ref = refs[:3]
    (
        chance_ref,
        dot_ref,
        peak_ref,
        dk_ref,
        dv_ref,
        dqt_ref,
        held_norm,
        held_turned,
        held_value,
        held_query,
        held_dq,
        cast_ref,
        gain_grad_ref,
        in_sem,
        dq_sem,
        out_sem,
    ) = refs[3:]
    half = half_ref[0]

    def loads(step):
        tiles = pl.ds(step * PAIRS, PAIRS)
        moves = [(queries_grads_ref.at[tiles], held_query.at[tiles])]
        for side in range(2):
            lanes = pl.ds(side * ROWS, ROWS)
            moves.append((norms[side].at[tiles], held_norm.at[tiles, side]))
            moves.append((turned[side].at[tiles], held_turned.at[tiles, :, lanes]))
            value = raws[0].at[tiles, 1] if side == 0 else raws[1].at[tiles]
            moves.append((value, held_value.at[tiles, side]))
        return [
            pltpu.make_async_copy(source, target, in_sem.at[step, index])
            for index, (source, target) in enumerate(moves)
        ]

    def dq_copy(block):
        shards = pl.ds(block * PAIRS, PAIRS)
        return pltpu.make_async_copy(
            held_dq.at[shards, :ROWS], dq_ref.at[shards, :ROWS], dq_sem.at[block]
        )

    for step in range(DEPTH // PAIRS):
        for copy in loads(step):
            copy.start()
    dk_ref[...] = jnp.zeros_like(dk_ref)
    dv_ref[...] = jnp.zeros_like(dv_ref)
    gain_grad_ref[...] = jnp.zeros_like(gain_grad_ref)

    def block_body(block, carry):
        for copy in loads(block):
            copy.wait()
        shards = [block * PAIRS + pair for pair in range(PAIRS)]
        unit_rows, inverse = unit_norm(
            jnp.concatenate([held_query[shard, 0] for shard in shards], axis=0)
        )
        query = (unit_rows * gain_ref[...]).astype(jnp.bfloat16)
        grad = jnp.concatenate([held_query[shard, 1] for shard in shards], axis=0)
        pos = pos_ref[pl.ds(block, 1), :]
        low = low_ref[pl.ds(block, 1), :]
        row = lax.broadcasted_iota(jnp.int32, (ROWS, LANES), 0)
        first, inner, diagonal, last = (bounds_ref[block, i] for i in range(4))

        def scores_body(masked, step, sums):
            best, total, weighted = sums
            parts = []
            peak = jnp.full((8, LANES), MASKED_SCORE, jnp.float32)
            for pair in range(PAIRS):
                tile = step * PAIRS + pair
                for side in range(2):
                    scores = nt_dot(held_norm[tile, side], query)
                    if masked:
                        which = half if side == 0 else 1 - half
                        base = (2 * tile + which) * ROWS
                        mask = row >= low - base
                        if masked > 1:
                            mask = mask & (row <= pos - base)
                        scores = jnp.where(mask, scores, MASKED_SCORE)
                    parts.append((tile, side, scores))
                    peak = jnp.maximum(peak, jnp.max(fold(scores), axis=0))
            new_best = jnp.maximum(best, jnp.max(peak, axis=0, keepdims=True) * EXP2_FACTOR)
            scale = jnp.exp2(best - new_best)
            total, weighted = total * scale, weighted * scale
            for index, (tile, side, scores) in enumerate(parts):
                shifted = jnp.exp2(scores * EXP2_FACTOR - new_best)
                dots = nt_dot(held_value[tile, side], grad)
                rows = slice(index * ROWS, (index + 1) * ROWS)
                chance_ref[step, rows] = shifted
                dot_ref[step, rows] = dots
                total = total + jnp.sum(fold(shifted), axis=0)
                weighted = weighted + jnp.sum(fold(shifted * dots), axis=0)
            peak_ref[pl.ds(step, 1), :] = new_best
            return new_best, total, weighted

        empty = jnp.zeros((8, LANES), jnp.float32)
        sums = (jnp.full((1, LANES), LEAST_PEAK, jnp.float32), empty, empty)
        sums = lax.fori_loop(first, inner, functools.partial(scores_body, 1), sums)
        sums = lax.fori_loop(inner, diagonal, functools.partial(scores_body, 0), sums)
        best, total, weighted = lax.fori_loop(
            diagonal, last, functools.partial(scores_body, 2), sums
        )
        share = 1.0 / jnp.sum(total, axis=0, keepdims=True)
        delta = jnp.sum(weighted, axis=0, keepdims=True) * share
        dqt_ref[...] = jnp.zeros_like(dqt_ref)

        def grads_body(step, carry):
            step_share = share * jnp.exp2(peak_ref[pl.ds(step, 1), :] - best)
            score_grads, keys_t = [], []
            for pair in range(PAIRS):
                rows = slice(pair * 2 * ROWS, (pair + 1) * 2 * ROWS)
                chance = chance_ref[step, rows] * step_share
                score_grad = (chance * (dot_ref[step, rows] - delta)).astype(jnp.bfloat16)
                dv_ref[step, rows] += nn_dot(chance.astype(jnp.bfloat16), grad)
                dk_ref[step, rows] += nn_dot(score_grad, query)
                score_grads.append(score_grad)
                keys_t.append(held_turned[step * PAIRS + pair])
            dqt_ref[...] += nn_dot(jnp.concatenate(keys_t, axis=1), jnp.concatenate(score_grads, axis=0))
            return carry

        lax.fori_loop(first, last, grads_body, 0)
        query_grad = dqt_ref[...].T * FACTOR
        raw_grad = unit_norm_backward(query_grad, unit_rows, inverse, gain_ref[...])
        for pair, shard in enumerate(shards):
            rows = slice(pair * ROWS, (pair + 1) * ROWS)
            held_dq[shard, :ROWS] = raw_grad[rows].astype(jnp.bfloat16)
        dq_copy(block).start()
        gain_grad_ref[...] += jnp.sum(query_grad * unit_rows, axis=0, keepdims=True)
        return carry

    lax.fori_loop(0, DEPTH // PAIRS, block_body, 0)
    copies = []
    for tile in range(DEPTH):
        step, base = tile // PAIRS, tile % PAIRS * 2 * ROWS
        for side, out_ref in enumerate((own_ref, other_ref)):
            rows = slice(base + side * ROWS, base + (side + 1) * ROWS)
            cast_ref[side, tile, 0] = dv_ref[step, rows].astype(jnp.bfloat16)
            cast_ref[side, tile, 1] = dk_ref[step, rows].astype(jnp.bfloat16)
            copies.append(
                pltpu.make_async_copy(
                    cast_ref.at[side, tile], out_ref.at[tile], out_sem.at[side, tile]
                )
            )
            copies[-1].start()
    key_total = jnp.zeros((ROWS, HD), jnp.float32)
    for tile in range(DEPTH):
        for side in range(2):
            start = (tile % PAIRS * 2 + side) * ROWS
            key_grad = dk_ref[tile // PAIRS, start : start + ROWS]
            key_total += key_grad * held_norm[tile, side].astype(jnp.float32)
    key_total = jnp.sum(key_total, axis=0, keepdims=True) * FACTOR / key_gain_ref[...]
    row = lax.broadcasted_iota(jnp.int32, (EXTRA, HD), 0)
    extra = jnp.zeros((EXTRA, HD), jnp.float32)
    for which, rest in enumerate((gain_grad_ref[...], key_total)):
        for index in range(3):
            term = rest.astype(jnp.bfloat16).astype(jnp.float32)
            extra = jnp.where(row == 3 * which + index, term, extra)
            rest = rest - term
    for tile in range(DEPTH):
        held_dq[tile, ROWS:] = extra.astype(jnp.bfloat16)
    copies.append(
        pltpu.make_async_copy(
            held_dq.at[:, ROWS:], dq_ref.at[:, ROWS:], dq_sem.at[DEPTH // PAIRS]
        )
    )
    copies[-1].start()
    for block in range(DEPTH // PAIRS):
        dq_copy(block).wait()
    for copy in copies:
        copy.wait()


def attention(bounds, half, pos, low, gain, key_gain, queries_grads, keys, raws):
    steps = DEPTH // PAIRS
    pairs = DEPTH * DEPTH * ROWS * 2 * ROWS
    scores = pltpu.VMEM((steps, WIDE, LANES), jnp.float32)
    total = pltpu.VMEM((steps, WIDE, HD), jnp.float32)
    both = pltpu.VMEM((DEPTH, 2, ROWS, HD), jnp.bfloat16)
    sums = jax.ShapeDtypeStruct((DEPTH, 2, ROWS, HD), jnp.bfloat16)
    return pl.pallas_call(
        attention_kernel,
        in_specs=[SMEM_SPEC, SMEM_SPEC] + [VMEM_SPEC] * 4 + [ANY_SPEC] * 7,
        out_specs=[ANY_SPEC, ANY_SPEC, ANY_SPEC],
        out_shape=[
            jax.ShapeDtypeStruct((DEPTH, ROWS + EXTRA, HD), jnp.bfloat16),
            sums,
            sums,
        ],
        scratch_shapes=[
            scores, scores, pltpu.VMEM((DEPTH, LANES), jnp.float32), total, total,
            pltpu.VMEM((HD, LANES), jnp.float32),
            both,
            pltpu.VMEM((DEPTH, HD, 2 * ROWS), jnp.bfloat16),
            both,
            both,
            pltpu.VMEM((DEPTH, ROWS + EXTRA, HD), jnp.bfloat16),
            pltpu.VMEM((2, DEPTH, 2, ROWS, HD), jnp.bfloat16),
            pltpu.VMEM((1, HD), jnp.float32),
            pltpu.SemaphoreType.DMA((steps, 7)),
            pltpu.SemaphoreType.DMA((DEPTH // PAIRS + 1,)),
            pltpu.SemaphoreType.DMA((2, DEPTH)),
        ],
        compiler_params=pltpu.CompilerParams(vmem_limit_bytes=VMEM_LIMIT),
        cost_estimate=pl.CostEstimate(
            flops=12 * pairs * HD, bytes_accessed=2**23, transcendentals=pairs
        ),
        name="attention",
    )(
        bounds, half, pos, low, gain, key_gain, queries_grads,
        *[key[0] for key in keys], *[key[1] for key in keys], *raws,
    )


def keys_of_pair():
    return pl.BlockSpec((DEPTH, 1, ROWS, HD), lambda i: (0, 0, 0, 0))


def finish_kernel(
    own_ref, other_ref, raw_ref, gain_ref, out_ref
):
    for tile in range(DEPTH):
        value_sum = own_ref[tile, 0].astype(jnp.float32) + other_ref[tile, 0].astype(jnp.float32)
        out_ref[tile, :ROWS] = value_sum.astype(jnp.bfloat16)
        grad_norm = own_ref[tile, 1].astype(jnp.float32) + other_ref[tile, 1].astype(jnp.float32)
        grad_norm = grad_norm * FACTOR
        unit_rows, inverse = unit_norm(raw_ref[tile, 0])
        out_ref[tile, ROWS : 2 * ROWS] = unit_norm_backward(
            grad_norm, unit_rows, inverse, gain_ref[...]
        ).astype(jnp.bfloat16)


def finish(own, other, raw, gain):
    rows = 2 * ROWS
    return pl.pallas_call(
        finish_kernel,
        grid=(1,),
        in_specs=[whole(DEPTH, 2, ROWS, HD), whole(DEPTH, 2, ROWS, HD)]
        + [keys_of_pair(), whole(1, HD)],
        out_specs=whole(DEPTH, rows, HD),
        out_shape=jax.ShapeDtypeStruct((DEPTH, rows, HD), jnp.bfloat16),
        cost_estimate=pl.CostEstimate(flops=0, bytes_accessed=2**23, transcendentals=0),
        compiler_params=pltpu.CompilerParams(vmem_limit_bytes=16 * 1024 * 1024),
        name="finish",
    )(own, other, raw, gain)


def project_kernel(part_ref, rows_ref, weight_ref, *refs):
    outs, (gains_ref, joined_ref) = refs[:-2], refs[-2:]
    width = outs[0].shape[1]
    for head in range(rows_ref.shape[0]):
        joined_ref[:, head * HD : (head + 1) * HD] = rows_ref[head, :ROWS]
        terms = rows_ref[head, ROWS:].astype(jnp.float32)
        for which in range(2):
            first, second, third = (terms[3 * which + i : 3 * which + i + 1] for i in range(3))
            place = which * HEADS_LOCAL + head
            gains_ref[place : place + 1, :] = (third + second) + first
    for step, out_ref in enumerate(outs):
        base = lax.rem(part_ref[0] + step, len(outs)) * width
        for start in range(0, width, COLUMNS):
            rows = pl.ds(pl.multiple_of(base + start, COLUMNS), COLUMNS)
            out_ref[:, start : start + COLUMNS] = nt_dot(
                joined_ref[...], weight_ref[rows, :]
            ).astype(jnp.bfloat16)


def project(part, weight, rows, parts):
    model, inner = weight.shape
    out = jax.ShapeDtypeStruct((ROWS, model // parts), jnp.bfloat16)
    return pl.pallas_call(
        project_kernel,
        in_specs=[SMEM_SPEC, VMEM_SPEC, VMEM_SPEC],
        out_specs=[VMEM_SPEC] * (parts + 1),
        out_shape=[out] * parts + [jax.ShapeDtypeStruct((2 * HEADS_LOCAL, HD), jnp.float32)],
        scratch_shapes=[pltpu.VMEM((ROWS, inner), jnp.bfloat16)],
        compiler_params=pltpu.CompilerParams(vmem_limit_bytes=20 * 1024 * 1024),
        cost_estimate=pl.CostEstimate(
            flops=2 * ROWS * model * inner, bytes_accessed=2 * model * inner, transcendentals=0
        ),
        name="project",
    )(part, rows, weight)


def along_z(pieces):
    return lax.all_to_all(pieces, "ctx", 0, 0, axis_index_groups=Z_GROUPS)


def swap_half(piece):
    return lax.ppermute(piece, "ctx", HALF_SWAP)


def sum_tp(parts):
    count = len(parts)
    total = parts[0].astype(jnp.float32)
    for step in range(1, count):
        pairs = [(index, (index + step) % count) for index in range(count)]
        total = total + lax.ppermute(parts[step], "tp", pairs).astype(jnp.float32)
    return total.astype(jnp.bfloat16)


def sum_gains(gains):
    moved = [
        lax.ppermute(gains, "dp", [(i, (i + step) % 4) for i in range(4)]) for step in (1, 2, 3)
    ]
    total = (gains + moved[1]) + (moved[0] + moved[2])
    return total + swap_half(total)


def local(q_raw, k_raw, values, d_out, q_gain, k_gain, q_weight, doc_lengths):
    ctx = lax.axis_index("ctx")
    z = ctx // 2
    half = lax.rem(ctx, 2)
    lengths = doc_lengths[0]
    starts = jnp.cumsum(lengths) - lengths
    q_gain_row = lax.dynamic_slice_in_dim(q_gain, z, 1, 0)
    k_gain_row = lax.dynamic_slice_in_dim(k_gain, z, 1, 0)

    pos = (2 * jnp.arange(8, dtype=jnp.int32)[:, None] + half) * ROWS + jnp.arange(
        ROWS, dtype=jnp.int32
    )
    pos = pos.reshape(DEPTH // PAIRS, LANES)
    low = jnp.max(
        jnp.where(starts[None, None, :] <= pos[:, :, None], starts[None, None, :], 0), axis=2
    )
    wide = 2 * ROWS * PAIRS
    first = low[:, 0] // wide
    last = pos[:, -1] // wide + 1
    diagonal = jnp.clip(pos[:, 0] // wide, first, last)
    inner = jnp.clip((low[:, -1] + wide - 1) // wide, first, diagonal)
    bounds = jnp.stack([first, inner, diagonal, last], axis=1).astype(jnp.int32)

    own = along_z(pack(k_raw[0], values[0]))
    sent, own = lax.optimization_barrier((pack(q_raw[0], d_out[0]), own))
    queries_grads = along_z(sent)
    key_other = swap_half(own[:, 0])
    keys_own = key_prep(k_gain_row, own)
    value_own, key_other, *keys_own = lax.optimization_barrier(
        (own[:, 1], key_other, *keys_own)
    )
    value_other = swap_half(value_own)
    (norm_own, turned_own), (norm_other, turned_other) = (
        keys_own,
        key_prep(k_gain_row, key_other),
    )
    dq, sums, other_sums = attention(
        bounds,
        half.reshape(1),
        pos,
        low,
        q_gain_row,
        k_gain_row,
        queries_grads,
        ((norm_own, turned_own), (norm_other, turned_other)),
        (own, value_other),
    )

    returned = along_z(dq)
    moved = swap_half(other_sums)
    *parts, gains = project(lax.axis_index("tp").reshape(1), q_weight, returned, 4)
    moved, *parts = lax.optimization_barrier((moved, *parts))
    input_grad = sum_tp(parts)
    finished = finish(sums, moved, own, k_gain_row)
    gains, finished = lax.optimization_barrier((gains, finished))
    gains = sum_gains(gains)
    value_grad, key_grad = unpack(along_z(finished))
    return (input_grad[None], key_grad[None], value_grad[None], gains[:HEADS_LOCAL], gains[HEADS_LOCAL:])


def solution(mesh):
    return jax.shard_map(
        local,
        mesh=mesh,
        in_specs=(
            P("dp", "ctx", "tp"),
            P("dp", "ctx", "tp"),
            P("dp", "ctx", "tp"),
            P("dp", "ctx", "tp"),
            P("tp", None),
            P("tp", None),
            P(None, "tp"),
            P("dp", None),
        ),
        out_specs=(
            P("dp", "ctx", "tp"),
            P("dp", "ctx", "tp"),
            P("dp", "ctx", "tp"),
            P("tp", None),
            P("tp", None),
        ),
        check_vma=False,
    )
```
